32 devices in a mesh: pool: 2 (over x), pw: 16 (over z, y, core).
Axes of the slice: x: 2, y: 2, z: 4, core: 2. Of those that a mesh axis runs over, the one named last changes fastest.
Arguments:
- orbitals: float32 [2, 2, 2, 192, 192, 192], P('pool', None, None, 'pw'), may hold values from -6 to 6
- responses: float32 [2, 2, 2, 192, 192, 192], P('pool', None, None, 'pw'), may hold values from -6 to 6
- energies: float32 [2, 2], P('pool'), may hold values from -0.6 to 0.4
- weights: float32 [2], P('pool'), may hold values from 0.5 to 1.5
- potential: float32 [192, 192, 192], P(None, 'pw'), may hold values from -3 to 3
- perturbation: float32 [192, 192, 192], P(None, 'pw'), may hold values from 0.2 to 2
Outputs:
- new_responses: float32 [2, 2, 2, 192, 192, 192], P('pool', None, None, 'pw')
- response_density: float32 [192, 192, 192], P('pw')
The draws below stay inside these ranges and needn't reach their ends.
All inputs are finite; a program needn't handle non-finite values.
Results may differ from the reference program's by a relative error of at most 0.0003.
Values sent between devices are 32-bit elements; how exact they have to be, the bound alone decides.
No kernel may reach another device: no remote copies, remote signals or barrier semaphores. Data moves between devices by JAX's collectives and lax.ppermute only.
A program may use at most 192 MiB of HBM per device.

```python
import jax
import jax.numpy as jnp
from jax import lax

GRID = 192
BANDS = 2
KPTS = 2


def block_scale(own_key, dims, cuts, low, top_value):
    factor_of = 1.0
    for position, shards_of in cuts:
        draws = jax.random.uniform(jax.random.fold_in(jax.random.fold_in(own_key, 6), position), (shards_of,), jnp.float32, low / len(cuts), top_value / len(cuts))
        factor_of = factor_of * jnp.repeat(jnp.exp(draws), dims[position] // shards_of).reshape((-1,) + (1,) * (len(dims) - 1 - position))
    return factor_of


def scatter_about(own_key, dims, spread, limit, shards=(), held_as=jnp.bfloat16):
    entries = spread * jax.random.normal(own_key, dims, jnp.float32)
    if shards:
        entries = entries * block_scale(own_key, dims, shards, -0.22, 0.18)
    return jnp.clip(entries, -limit, limit).astype(held_as)


def setup_inputs(seed: int = 0) -> dict:
    streams_of = jax.random.split(jax.random.key(seed), 7)
    return {
        "orbitals": scatter_about(streams_of[0], (KPTS, BANDS, 2, GRID, GRID, GRID), 1.0, 6.0, ((0, 2), (3, 16)), jnp.float32),
        "responses": scatter_about(streams_of[1], (KPTS, BANDS, 2, GRID, GRID, GRID), 1.0, 6.0, ((0, 2), (3, 16)), jnp.float32),
        "energies": jnp.clip(-0.6 + 1 * jax.random.uniform(streams_of[2], (KPTS, BANDS), jnp.float32) ** block_scale(streams_of[2], (KPTS, BANDS), ((0, 2),), -0.2, 0.2), -0.6, 0.4),
        "weights": jnp.clip(0.5 + 1.0 * jax.random.uniform(streams_of[3], (KPTS,), jnp.float32) ** block_scale(streams_of[3], (KPTS,), ((0, 2),), -0.2, 0.2), 0.5, 1.5),
        "potential": jnp.clip(jax.random.uniform(streams_of[4], (GRID, GRID, GRID), jnp.float32, -3.0, 3.0) * block_scale(streams_of[4], (GRID, GRID, GRID), ((1, 16),), -0.4, 0.0), -3.0, 3.0),
        "perturbation": jnp.clip(0.2 + 1.8 * jax.random.uniform(streams_of[5], (GRID, GRID, GRID), jnp.float32) ** block_scale(streams_of[5], (GRID, GRID, GRID), ((1, 16),), -0.2, 0.2), 0.2, 2.0),
    }


RECIPROCAL_SQUARE = 0.023428
ORDERINGS = ((0, 1, 2), (1, 0, 2))


def negated(values, along_axis):
    return jnp.roll(jnp.flip(values, along_axis), 1, along_axis)


def reference(orbitals, responses, energies, weights, potential, perturbation):
    length = orbitals.shape[-1]
    frequency = jnp.arange(length, dtype=jnp.int32)
    frequency = jnp.where(frequency < length // 2, frequency, frequency - length).astype(jnp.float32)
    kinetic = 0.5 * RECIPROCAL_SQUARE * (frequency[:, None, None] * frequency[:, None, None] + frequency[None, :, None] * frequency[None, :, None] + frequency[None, None, :] * frequency[None, None, :])
    cell_count = float(length ** 3)
    density = jnp.zeros((length, length, length), jnp.float32)
    updated_all = []
    for kpoint in range(KPTS):
        residual_list = []
        for band_index in range(BANDS):
            orbital_space = jnp.fft.ifftn(lax.complex(orbitals[kpoint, band_index, 0], orbitals[kpoint, band_index, 1]), norm="ortho")
            response_space = jnp.fft.ifftn(lax.complex(responses[kpoint, band_index, 0], responses[kpoint, band_index, 1]), norm="ortho")
            density = density + 2.0 * weights[kpoint] * (orbital_space.real * response_space.real + orbital_space.imag * response_space.imag)
            applied_space = potential * response_space + perturbation * orbital_space
            applied = jnp.fft.fftn(applied_space, norm="ortho")
            shifted = kinetic - energies[kpoint, band_index]
            residual_real = shifted * responses[kpoint, band_index, 0] + applied.real
            residual_imag = shifted * responses[kpoint, band_index, 1] + applied.imag
            residual_list.append(jnp.stack((residual_real, residual_imag)))
        residual = jnp.stack(residual_list)
        left_real = orbitals[kpoint, :, 0].reshape(BANDS, -1)
        left_imag = orbitals[kpoint, :, 1].reshape(BANDS, -1)
        right_real = residual[:, 0].reshape(BANDS, -1)
        right_imag = residual[:, 1].reshape(BANDS, -1)
        highest = lax.Precision.HIGHEST
        over_real = jnp.dot(left_real, right_real.T, precision=highest) + jnp.dot(left_imag, right_imag.T, precision=highest)
        over_imag = jnp.dot(left_real, right_imag.T, precision=highest) - jnp.dot(left_imag, right_real.T, precision=highest)
        combine_real = jnp.dot(over_real.T, left_real, precision=highest) - jnp.dot(over_imag.T, left_imag, precision=highest)
        combine_imag = jnp.dot(over_imag.T, left_real, precision=highest) + jnp.dot(over_real.T, left_imag, precision=highest)
        combined = jnp.stack((combine_real, combine_imag), axis=1).reshape(residual.shape)
        projected = residual - combined / cell_count
        updated_all.append(responses[kpoint] - projected / (1.0 + kinetic))
    new_responses = jnp.stack(updated_all)
    summed = jnp.zeros_like(density)
    for pattern in range(4):
        flipped = density
        for along_axis in range(2):
            if (pattern >> along_axis) & 1:
                flipped = negated(flipped, along_axis)
        for ordering in ORDERINGS:
            summed = summed + jnp.transpose(flipped, ordering)
    return new_responses, summed / 8.0
```

```python
import functools
import math

import jax
import jax.numpy as jnp
import ml_dtypes
import numpy as np
from jax import lax
from jax.experimental import pallas as pl
from jax.experimental.pallas import tpu as pltpu
from jax.sharding import PartitionSpec as P

RECIPROCAL_SQUARE = 0.023428
VMEM_BYTES = 56 * 1024 * 1024


def split_table(table):
    high = table.astype(ml_dtypes.bfloat16)
    low = (table - high.astype(np.float64)).astype(ml_dtypes.bfloat16)
    return np.stack((high, low))


@functools.cache
def matrices(length, slab, members):
    index = np.arange(length)
    angles = (index[:, None] * index[None, :] % length) * (2.0 * math.pi / length)
    cosine = np.cos(angles) / math.sqrt(length)
    sine = np.sin(angles) / math.sqrt(length)
    lanes = 128 * -(-length // 128)
    pad = ((0, 0), (0, lanes - length))
    inverse = np.block([[cosine, -sine], [sine, cosine]])
    forward = np.block([[cosine, sine], [-sine, cosine]])
    sent = np.arange(2 * length).reshape(2, members, slab).transpose(1, 0, 2).reshape(-1)
    got = np.arange(2 * length).reshape(2, members, slab // 2, 2).transpose(0, 3, 1, 2).reshape(-1)
    mirror = np.eye(length) + np.eye(length)[(-index) % length]
    both = np.zeros((members, 2, slab, 2, length))
    for which in range(2):
        both[:, which, :, which, :] = mirror.reshape(members, slab, length)
    return {
        "cosine": split_table(np.pad(cosine, pad)),
        "sine": split_table(np.pad(sine, pad)),
        "inverse_send": split_table(inverse[sent]),
        "inverse_receive": split_table(inverse[:, got]),
        "forward_send": split_table(forward[sent]),
        "forward_receive": split_table(forward[:, got]),
        "mirror_pair": both.reshape(2 * length, 2 * length).astype(ml_dtypes.bfloat16),
    }


def halves(values):
    high = values.astype(jnp.bfloat16)
    return high, (values - high.astype(jnp.float32)).astype(jnp.bfloat16)


def dot(left, right):
    return lax.dot_general(
        left, right, (((1,), (0,)), ((), ())), preferred_element_type=jnp.float32
    )


def dot_right(values, table):
    high, low = halves(values)
    return dot(high, table[0]) + (dot(high, table[1]) + dot(low, table[0]))


def dot_left(table, values):
    high, low = halves(values)
    return dot(table[0], high) + (dot(table[0], low) + dot(table[1], high))


def dot_mirror(table, values):
    high, low = halves(values)
    low_rest = (values - high.astype(jnp.float32) - low.astype(jnp.float32)).astype(jnp.bfloat16)
    return dot(table, high) + (dot(table, low) + dot(table, low_rest))


def merge_tails(first, second):
    return first + pltpu.roll(second, 64, 1)


def to_half_kernel(field, cosine, sine, send, out):
    pair, length = field.shape[3], field.shape[4]
    members, rows = out.shape[0], out.shape[3]
    values = field[...].reshape(2 * pair * length, length)
    by_cos = dot_right(values, cosine)
    by_sin = dot_right(values, sine)
    mid = pair * length
    real = by_cos[:mid] - by_sin[mid:]
    imag = by_sin[:mid] + by_cos[mid:]
    tails = []
    for one in range(pair):
        part = slice(one * length, (one + 1) * length)
        done = dot_left(send, jnp.concatenate((real[part], imag[part]), axis=0))
        out[:, 0, one] = done[:, :128].reshape(members, rows, 128)
        tails.append(done[:, 128:])
    out[:, 0, 2] = merge_tails(*tails).reshape(members, rows, 128)


def received(ref, start, stride, count):
    return ref[pl.ds(start, count, stride=stride), :]


def plane(got, chunks, place, slab, count, with_main, with_tail):
    stride = chunks * 2 * slab
    found = []
    for part in range(2):
        row = part * slab + place
        if with_main:
            mains = [received(got, one * 2 * slab + row, stride, count) for one in range(2)]
        if with_tail:
            tail = received(got, (chunks - 1) * 2 * slab + row, stride, count)
            tails = [tail, pltpu.roll(tail, 64, 1)]
        for one in range(2):
            pieces = ([mains[one]] if with_main else []) + ([tails[one]] if with_tail else [])
            found.append(jnp.concatenate(pieces, axis=1) if len(pieces) > 1 else pieces[0])
    return jnp.concatenate(found, axis=0)


def to_space_kernel(slab, got, receive, space):
    count = got.shape[0] // (6 * slab)
    for one in range(2):
        place = 2 * pl.program_id(0) + one
        values = plane(got, 3, place, slab, count, True, True)
        space[one] = dot_left(receive, values)[:, : space.shape[2]]


def folded(values):
    return values.reshape(-1, 8, values.shape[-1]).sum(axis=0)


def apply_kernel(
    slab, band, weights, got, spaces, potential, perturbation, before,
    receive, cosine, sine, send, mirror, out_main, out_tail, inner, density, *high_half
):
    length = potential.shape[1]
    members, rows = out_main.shape[0], out_main.shape[3]
    count = got.shape[0] // (6 * slab)
    step = pl.program_id(0)
    twice_weight = 2.0 * weights[0]

    @pl.when(step == 0)
    def _():
        inner[...] = jnp.zeros_like(inner)

    tails = []
    sums = []
    for one in range(2):
        values = plane(got, 3, 2 * step + one, slab, count, True, True)
        response = dot_left(receive, values)[:, :length]
        real, imag = response[:length], response[length:]
        own_real, own_imag = spaces[band, one, :length], spaces[band, one, length:]
        local = twice_weight * (own_real * real + own_imag * imag)
        if before is not None:
            local = local + before[one]
        sums.append(local)
        field, change = potential[one], perturbation[one]
        real = field * real + change * own_real
        imag = field * imag + change * own_imag
        for other in range(2):
            left_real, left_imag = spaces[other, one, :length], spaces[other, one, length:]
            inner[0, other] += folded(left_real * real + left_imag * imag)
            inner[1, other] += folded(left_real * imag - left_imag * real)
        both = jnp.concatenate((real, imag), axis=0)
        by_cos = dot_right(both, cosine)
        by_sin = dot_right(both, sine)
        turned = jnp.concatenate(
            (by_cos[:length] + by_sin[length:], by_cos[length:] - by_sin[:length]), axis=0
        )
        done = dot_left(send, turned)
        out_main[:, 0, one] = done[:, :128].reshape(members, rows, 128)
        tails.append(done[:, 128:])
    tail = merge_tails(*tails).reshape(members, rows, 128)
    if out_tail is None:
        out_main[:, 0, 2] = tail
    else:
        out_tail[:, 0] = tail
    if not high_half:
        for one in range(2):
            density[one] = sums[one]
        return
    summed = dot_mirror(mirror[...], jnp.concatenate(sums, axis=0))
    density[...] = summed[:, :128].reshape(density.shape)
    half = length // 2
    lanes = jnp.concatenate((summed[:, half:], summed[:, :half]), axis=1)[:, :128]
    high_half[0][...] = lanes.reshape(density.shape)


def frequencies(length, first, lanes, first_lane):
    rows = lax.broadcasted_iota(jnp.int32, (length, lanes), 0)
    columns = lax.broadcasted_iota(jnp.int32, (length, lanes), 1) + first_lane
    row = jnp.where(rows < length // 2, rows, rows - length).astype(jnp.float32)
    column = jnp.where(columns < length // 2, columns, columns - length).astype(jnp.float32)
    outer = jnp.where(first < length // 2, first, first - length).astype(jnp.float32)
    return 0.5 * RECIPROCAL_SQUARE * (outer * outer + row * row + column * column)


def inner_kernel(slab, me, energies, orbitals, responses, inner):
    length = orbitals.shape[4]
    step = pl.program_id(0)

    @pl.when(step == 0)
    def _():
        inner[...] = jnp.zeros_like(inner)

    for one in range(2):
        kinetic = frequencies(length, me[0] * slab + 2 * step + one, length, 0)
        for band in range(2):
            shifted = kinetic - energies[0, band]
            real = shifted * responses[0, band, 0, one]
            imag = shifted * responses[0, band, 1, one]
            for other in range(2):
                left_real, left_imag = orbitals[0, other, 0, one], orbitals[0, other, 1, one]
                inner[0, other, band] += folded(left_real * real + left_imag * imag)
                inner[1, other, band] += folded(left_real * imag - left_imag * real)


def direct_kernel(slab, me, energies, inner, orbitals, responses, out):
    length = orbitals.shape[4]
    cells = float(length**3)
    for one in range(2):
        kinetic = frequencies(length, me[0] * slab + 2 * pl.program_id(0) + one, length, 0)
        inverse = 1.0 / (1.0 + kinetic)
        for band in range(2):
            shifted = kinetic - energies[0, band]
            real = shifted * responses[0, band, 0, one]
            imag = shifted * responses[0, band, 1, one]
            for other in range(2):
                left_real, left_imag = orbitals[0, other, 0, one], orbitals[0, other, 1, one]
                by_real = inner[0, other, band] / cells
                by_imag = inner[1, other, band] / cells
                real = real - (left_real * by_real - left_imag * by_imag)
                imag = imag - (left_real * by_imag + left_imag * by_real)
            out[0, band, 0, one] = responses[0, band, 0, one] - real * inverse
            out[0, band, 1, one] = responses[0, band, 1, one] - imag * inverse


def finish_kernel(slab, chunks, tail, me, got, receive, base, out):
    length = base.shape[4]
    count = got.shape[0] // (chunks * 2 * slab)
    for one in range(2):
        place = 2 * pl.program_id(0) + one
        values = plane(got, chunks, place, slab, count, not tail, tail)
        applied = dot_left(receive, values)
        kinetic = frequencies(length, me[0] * slab + place, 128, 128 if tail else 0)
        inverse = 1.0 / (1.0 + kinetic)
        for part in range(2):
            piece = applied[part * length : (part + 1) * length]
            out[0, 0, part, one] = base[0, 0, part, one] - piece * inverse


def mirror_kernel(slab, got, mirror, single, out, natural):
    length = natural.shape[1]
    planes = [
        received(got, 2 * pl.program_id(0) + one, slab, length) for one in range(2)
    ]
    out[...] = dot_mirror(mirror[...], jnp.concatenate(planes, axis=0)).reshape(out.shape)
    for one in range(2):
        natural[one] = dot_mirror(single[...], planes[one])


def swap_kernel(slab, got, natural, out):
    length = natural.shape[1]
    for one in range(2):
        swapped = received(got, 2 * pl.program_id(0) + one, slab, length)
        out[one] = (natural[one] + swapped) * 0.125


def cost(flops, moved):
    return pl.CostEstimate(flops=int(flops), bytes_accessed=int(moved), transcendentals=0)


def whole():
    return pl.BlockSpec(memory_space=pltpu.VMEM)


def scalars():
    return pl.BlockSpec(memory_space=pltpu.SMEM)


def call(kernel, name, grid, ins, outs, shapes, estimate, aliases=None):
    return pl.pallas_call(
        kernel,
        grid=(grid,),
        in_specs=ins,
        out_specs=outs,
        out_shape=shapes,
        compiler_params=pltpu.CompilerParams(
            dimension_semantics=("arbitrary",), vmem_limit_bytes=VMEM_BYTES
        ),
        cost_estimate=estimate,
        input_output_aliases=aliases or {},
        name=name,
    )


def f32(*shape):
    return jax.ShapeDtypeStruct(shape, jnp.float32)


def packed_body(orbitals, responses, energies, weights, potential, perturbation):
    length = orbitals.shape[-1]
    slab = orbitals.shape[3]
    members = length // slab
    pairs = slab // 2
    rows = 2 * slab
    half = length // 2
    table = {key: jnp.asarray(value) for key, value in matrices(length, slab, members).items()}
    single = jnp.asarray(
        (np.eye(length) + np.eye(length)[(-np.arange(length)) % length]).astype(ml_dtypes.bfloat16)
    )
    me = lax.axis_index("pw").astype(jnp.int32).reshape(1)
    pool = lax.axis_index("pool")
    flat = (members * pairs * 3 * rows, 128)
    field_bytes = 4 * members * pairs * 3 * rows * 128
    stage_flops = 6 * 2 * 2 * length * length * length * slab * 2

    half_spec = pl.BlockSpec((members, 1, 3, rows, 128), lambda p: (0, p, 0, 0, 0))
    half_shape = f32(members, pairs, 3, rows, 128)

    def exchange(values, after=None):
        values = values.reshape(members, -1, 128)
        if after is not None:
            values, _ = lax.optimization_barrier((values, after))
        return lax.all_to_all(values, "pw", split_axis=0, concat_axis=0, tiled=True)

    def to_half(field, band):
        return call(
            to_half_kernel,
            "to_half",
            pairs,
            [
                pl.BlockSpec((1, 1, 2, 2, length, length), lambda p: (0, band, 0, p, 0, 0)),
                whole(),
                whole(),
                whole(),
            ],
            half_spec,
            half_shape,
            cost(2 * stage_flops, 2 * field_bytes),
        )(field, table["cosine"], table["sine"], table["inverse_send"])

    def to_space(got):
        return call(
            functools.partial(to_space_kernel, slab),
            "to_space",
            pairs,
            [whole(), whole()],
            pl.BlockSpec((2, 2 * length, length), lambda p: (p, 0, 0)),
            f32(slab, 2 * length, length),
            cost(stage_flops, 2 * field_bytes),
        )(got.reshape(flat), table["inverse_receive"])

    plane_spec = pl.BlockSpec((2, length, length), lambda p: (p, 0, 0))
    send_specs = [
        pl.BlockSpec((members, 1, 2, rows, 128), lambda p: (0, p, 0, 0, 0)),
        pl.BlockSpec((members, 1, rows, 128), lambda p: (0, p, 0, 0)),
    ]
    send_shapes = [
        f32(members, pairs, 2, rows, 128),
        f32(members, pairs, rows, 128),
    ]
    density_spec = pl.BlockSpec((members, 2 * slab, 128), lambda p: (0, p, 0))
    density_shape = f32(members, slab * slab, 128)
    inner_spec = pl.BlockSpec((2, 2, 8, length), lambda p: (0, 0, 0, 0))

    def apply_first(got, spaces, field, change):
        def kernel(weights, got, first, second, field, change, *tables_and_outs):
            receive, cosine, sine, send, main, inner, density = tables_and_outs
            apply_kernel(
                slab, 0, weights, got, Both(first, second), field, change, None,
                receive, cosine, sine, send, None, main, None, inner, density,
            )

        return call(
            kernel,
            "apply_first",
            pairs,
            [scalars(), whole(), space_spec, space_spec, plane_spec, plane_spec] + [whole()] * 4,
            [half_spec, inner_spec, plane_spec],
            [half_shape, f32(2, 2, 8, length), f32(slab, length, length)],
            cost(3 * stage_flops, 5 * field_bytes),
        )(
            weights, got.reshape(flat), *spaces, field, change,
            table["inverse_receive"], table["cosine"], table["sine"], table["forward_send"],
        )

    def apply_last(got, spaces, field, change, before):
        def kernel(weights, got, first, second, field, change, before, *tables_and_outs):
            receive, cosine, sine, send, mirror, main, tail, inner, low, high = tables_and_outs
            apply_kernel(
                slab, 1, weights, got, Both(first, second), field, change, before,
                receive, cosine, sine, send, mirror, main, tail, inner, low, high,
            )

        return call(
            kernel,
            "apply_last",
            pairs,
            [scalars(), whole(), space_spec, space_spec] + [plane_spec] * 3 + [whole()] * 5,
            send_specs + [inner_spec, density_spec, density_spec],
            send_shapes + [f32(2, 2, 8, length), density_shape, density_shape],
            cost(3 * stage_flops, 5 * field_bytes),
        )(
            weights, got.reshape(flat), *spaces, field, change, before,
            table["inverse_receive"], table["cosine"], table["sine"], table["forward_send"],
            table["mirror_pair"],
        )

    space_spec = pl.BlockSpec((2, 2 * length, length), lambda p: (p, 0, 0))
    bands_spec = pl.BlockSpec((1, 2, 2, 2, length, length), lambda p: (0, 0, 0, p, 0, 0))

    def finish(base, got, band, chunks, tail):
        lane_block = 1 if tail else 0
        one_spec = pl.BlockSpec(
            (1, 1, 2, 2, length, 128), lambda p: (0, band, 0, p, 0, lane_block)
        )
        return call(
            functools.partial(finish_kernel, slab, chunks, tail),
            "finish",
            pairs,
            [scalars(), whole(), whole(), one_spec],
            one_spec,
            f32(*base.shape),
            cost(stage_flops, 2 * field_bytes),
            {3: 0},
        )(me, got.reshape(-1, 128), table["forward_receive"], base)

    field = jnp.transpose(potential, (1, 0, 2))
    change = jnp.transpose(perturbation, (1, 0, 2))
    got_one = exchange(to_half(orbitals, 0))
    got_two = exchange(to_half(orbitals, 1), got_one)
    got_first = exchange(to_half(responses, 0), got_two)
    direct_inner = call(
        functools.partial(inner_kernel, slab),
        "inner",
        pairs,
        [scalars(), scalars(), bands_spec, bands_spec],
        pl.BlockSpec((2, 2, 2, 8, length), lambda p: (0, 0, 0, 0, 0)),
        f32(2, 2, 2, 8, length),
        cost(32 * field_bytes, 4 * field_bytes),
    )(me, energies, orbitals, responses)
    got_last = exchange(to_half(responses, 1), (got_first, direct_inner))
    spaces = [to_space(got_one), to_space(got_two)]
    send_first, inner_first, before = apply_first(got_first, spaces, field, change)
    back_first = exchange(send_first, got_last)
    last_main, last_tail, inner_last, low, high = apply_last(
        got_last, spaces, field, change, before
    )
    kept = jnp.where(pool == 0, low, high)
    given = jnp.where(pool == 0, high, low)
    swap = [(0, 1), (1, 0)]
    local_inner = direct_inner + jnp.stack((inner_first, inner_last), axis=2)
    local_inner = jnp.sum(local_inner, axis=(3, 4)).reshape(8)
    riding = jnp.pad(local_inner, (0, slab * slab - 8)).reshape(1, -1, 1)
    used = lax.broadcasted_iota(jnp.int32, density_shape.shape, 2) < half
    summed = jnp.where(used, kept + lax.ppermute(given, "pool", swap), riding)
    got_density = exchange(summed, back_first)
    inner = jnp.sum(got_density[:, :8, half], axis=0).reshape(2, 2, 2)
    back_tail = exchange(last_tail, got_density)
    base = call(
        functools.partial(direct_kernel, slab),
        "direct",
        pairs,
        [scalars(), scalars(), scalars(), bands_spec, bands_spec],
        bands_spec,
        f32(*responses.shape),
        cost(32 * field_bytes, 6 * field_bytes),
    )(me, energies, inner, orbitals, responses)
    natural_spec = pl.BlockSpec((2, length, 128), lambda p: (p, 0, 0))
    mirrored, natural = call(
        functools.partial(mirror_kernel, slab),
        "mirror",
        pairs,
        [whole(), whole(), whole()],
        [density_spec, natural_spec],
        [density_shape, f32(slab, length, 128)],
        cost(2e9, 4e6),
    )(got_density.reshape(-1, 128), table["mirror_pair"], single)
    got_mirrored = exchange(mirrored, (back_tail, base))
    base = finish(base, back_first, 0, 3, False)
    base = finish(base, back_first, 0, 3, True)
    back_main = exchange(last_main, (got_mirrored, base))
    symmetric = call(
        functools.partial(swap_kernel, slab),
        "swap",
        pairs,
        [whole(), natural_spec],
        natural_spec,
        f32(slab, length, 128),
        cost(1e6, 4e6),
    )(got_mirrored.reshape(-1, 128), natural)
    other = lax.ppermute(symmetric, "pool", swap)
    kept, other = symmetric[..., :half], other[..., :half]
    response_density = jnp.where(
        pool == 0,
        jnp.concatenate((kept, other), axis=2),
        jnp.concatenate((other, kept), axis=2),
    )
    base = finish(base, back_tail, 1, 1, True)
    base, response_density, back_main = lax.optimization_barrier(
        (base, response_density, back_main)
    )
    base = finish(base, back_main, 1, 2, False)
    return base, response_density


class Both:
    def __init__(self, *refs):
        self.refs = refs

    def __getitem__(self, index):
        return self.refs[index[0]][index[1:]]


def tables(length):
    indices = jnp.arange(length, dtype=jnp.int32)
    angles = (indices[:, None] * indices[None, :] % length).astype(jnp.float32) * (
        2.0 * math.pi / length
    )
    factor = 1.0 / math.sqrt(length)
    return (jnp.cos(angles) * factor, jnp.sin(angles) * factor)


def apply_table(values, table_in, along_axis):
    rotated = jnp.tensordot(
        values, table_in, axes=((along_axis,), (0,)), precision=lax.Precision.HIGHEST
    )
    return jnp.moveaxis(rotated, -1, along_axis)


def transform(field_in, along_axis, cosine_table, sine_table, phase_sign):
    real_part = field_in[:, :, 0]
    imag_part = field_in[:, :, 1]
    real_cos = apply_table(real_part, cosine_table, along_axis)
    real_sin = apply_table(real_part, sine_table, along_axis)
    imag_cos = apply_table(imag_part, cosine_table, along_axis)
    imag_sin = apply_table(imag_part, sine_table, along_axis)
    return jnp.stack((real_cos - phase_sign * imag_sin, phase_sign * real_sin + imag_cos), axis=2)


def signed_freq(indices, length):
    return jnp.where(indices < length // 2, indices, indices - length).astype(jnp.float32)


def negated(values, along_axis):
    return jnp.roll(jnp.flip(values, along_axis), 1, along_axis)


def products(left_side, right_side):
    band_count = left_side.shape[0]
    highest = lax.Precision.HIGHEST
    left_real = left_side[:, 0].reshape(band_count, -1)
    left_imag = left_side[:, 1].reshape(band_count, -1)
    right_real = right_side[:, 0].reshape(band_count, -1)
    right_imag = right_side[:, 1].reshape(band_count, -1)
    real_sum = jnp.dot(left_real, right_real.T, precision=highest) + jnp.dot(
        left_imag, right_imag.T, precision=highest
    )
    imag_sum = jnp.dot(left_real, right_imag.T, precision=highest) - jnp.dot(
        left_imag, right_real.T, precision=highest
    )
    return (real_sum, imag_sum)


def plain_body(orbitals, responses, energies, weights, potential, perturbation):
    length = orbitals.shape[-1]
    slab_rows = orbitals.shape[3]
    cosine_table, sine_table = tables(length)

    def to_space(field_in):
        return transform(
            transform(field_in, 4, cosine_table, sine_table, 1.0), 3, cosine_table, sine_table, 1.0
        )

    def finish_one(one_piece):
        return transform(one_piece, 2, cosine_table, sine_table, 1.0)

    orbital_space = finish_one(
        lax.all_to_all(to_space(orbitals), "pw", split_axis=4, concat_axis=3, tiled=True)
    )
    response_space = finish_one(
        lax.all_to_all(to_space(responses), "pw", split_axis=4, concat_axis=3, tiled=True)
    )
    partial_value = (
        2.0
        * weights[0]
        * jnp.sum(
            orbital_space[0, :, 0] * response_space[0, :, 0]
            + orbital_space[0, :, 1] * response_space[0, :, 1],
            axis=0,
        )
    )
    applied_space = potential * response_space + perturbation * orbital_space
    first_row = lax.axis_index("pw") * slab_rows
    row_freq = signed_freq(first_row + jnp.arange(slab_rows, dtype=jnp.int32), length)
    full_freq = signed_freq(jnp.arange(length, dtype=jnp.int32), length)
    kinetic = (
        0.5
        * RECIPROCAL_SQUARE
        * (
            row_freq[:, None, None] * row_freq[:, None, None]
            + full_freq[None, :, None] * full_freq[None, :, None]
            + full_freq[None, None, :] * full_freq[None, None, :]
        )
    )
    shifted = kinetic[None] - energies[0][:, None, None, None]
    direct = shifted[None, :, None] * responses
    sectioned = transform(
        transform(applied_space, 4, cosine_table, sine_table, -1.0),
        2,
        cosine_table,
        sine_table,
        -1.0,
    )
    residual = direct + transform(
        lax.all_to_all(sectioned, "pw", split_axis=3, concat_axis=4, tiled=True),
        3,
        cosine_table,
        sine_table,
        -1.0,
    )
    over_real, over_imag = lax.psum(products(orbitals[0], residual[0]), "pw")
    highest = lax.Precision.HIGHEST
    orbital_real = orbitals[0, :, 0]
    orbital_imag = orbitals[0, :, 1]
    combine_real = jnp.einsum(
        "mn,mxyz->nxyz", over_real, orbital_real, precision=highest
    ) - jnp.einsum("mn,mxyz->nxyz", over_imag, orbital_imag, precision=highest)
    combine_imag = jnp.einsum(
        "mn,mxyz->nxyz", over_imag, orbital_real, precision=highest
    ) + jnp.einsum("mn,mxyz->nxyz", over_real, orbital_imag, precision=highest)
    cell_count = float(length**3)
    projected = residual - jnp.stack((combine_real, combine_imag), axis=1)[None] / cell_count
    new_responses = responses - projected / (1.0 + kinetic)[None, None, None]
    summed = lax.psum(partial_value, "pool")
    mirrored = summed + negated(summed, 0)
    row_slab = lax.all_to_all(mirrored, "pw", split_axis=0, concat_axis=1, tiled=True)
    signsum = row_slab + negated(row_slab, 1)
    swapped = lax.all_to_all(signsum, "pw", split_axis=1, concat_axis=0, tiled=True)
    total_sym = signsum + jnp.transpose(swapped, (1, 0, 2))
    return (new_responses, total_sym / 8.0)


def body(orbitals, responses, energies, weights, potential, perturbation):
    slab, length = orbitals.shape[3], orbitals.shape[-1]
    fits = slab % 4 == 0 and length == 192 and orbitals.shape[0] == 1 and orbitals.shape[1] == 2
    return (packed_body if fits else plain_body)(
        orbitals, responses, energies, weights, potential, perturbation
    )


def solution(mesh):
    placed = (
        P("pool", None, None, "pw", None, None),
        P("pool", None, None, "pw", None, None),
        P("pool", None),
        P("pool"),
        P(None, "pw", None),
        P(None, "pw", None),
    )
    return jax.shard_map(
        body,
        mesh=mesh,
        in_specs=placed,
        out_specs=(P("pool", None, None, "pw", None, None), P("pw", None, None)),
        check_vma=False,
    )
```

```python
import functools
import math

import jax
import jax.numpy as jnp
import ml_dtypes
import numpy as np
from jax import lax
from jax.experimental import pallas as pl
from jax.experimental.pallas import tpu as pltpu
from jax.sharding import PartitionSpec as P

RECIPROCAL_SQUARE = 0.023428
VMEM_BYTES = 62 * 1024 * 1024


def split_table(table):
    high = table.astype(ml_dtypes.bfloat16)
    low = (table - high.astype(np.float64)).astype(ml_dtypes.bfloat16)
    return np.stack((high, low))


def long_table(table):
    high, low = split_table(table)
    return np.concatenate((high, high, low), axis=1)


@functools.cache
def matrices(length, slab, members):
    index = np.arange(length)
    angles = (index[:, None] * index[None, :] % length) * (2.0 * math.pi / length)
    cosine = np.cos(angles) / math.sqrt(length)
    sine = np.sin(angles) / math.sqrt(length)
    lanes = 128 * -(-length // 128)
    pad = ((0, 0), (0, lanes - length))
    inverse = np.block([[cosine, -sine], [sine, cosine]])
    forward = np.block([[cosine, sine], [-sine, cosine]])
    sent = np.arange(2 * length).reshape(2, members, slab).transpose(1, 0, 2).reshape(-1)
    got = np.arange(2 * length).reshape(2, members, slab // 2, 2).transpose(3, 0, 1, 2)
    got = got.reshape(2, -1)
    first = np.arange(2 * length).reshape(2, 2, length // 2)[:, 0].reshape(-1)
    parity = np.arange(2 * length).reshape(length, 2).T
    mirror = np.eye(length) + np.eye(length)[(-index) % length]
    both = np.zeros((members, 2, slab, 2, length))
    for which in range(2):
        both[:, which, :, which, :] = mirror.reshape(members, slab, length)
    both = both.reshape(2 * length, 2, length)
    alone = np.pad(mirror.reshape(members, slab, length), ((0, 0), (0, 4), (0, 0)))
    alone = alone.reshape(-1, length)
    loose = index.reshape(members, slab).T.reshape(-1)
    return {
        "cosine": split_table(np.pad(cosine, pad)),
        "mixed": np.stack(
            [split_table(np.pad(sine + sign * cosine, pad)) for sign in (-1.0, 1.0)]
        ),
        "inverse_send": np.stack([long_table(inverse[sent[:length]][:, one]) for one in parity]),
        "inverse_receive": np.stack([long_table(inverse[first][:, one]) for one in got]),
        "forward_send": long_table(forward[sent]),
        "forward_receive": np.stack([long_table(forward[first][:, one]) for one in got]),
        "pair": both.reshape(2 * length, -1).astype(ml_dtypes.bfloat16),
        "alone": alone.astype(ml_dtypes.bfloat16),
        "loose_pair": both[:, :, loose].reshape(2 * length, -1).astype(ml_dtypes.bfloat16),
        "loose_alone": alone[:, loose].astype(ml_dtypes.bfloat16),
        "loose_mirror": mirror[:, loose].astype(ml_dtypes.bfloat16),
        "loose_order": np.eye(length)[:, loose].astype(ml_dtypes.bfloat16),
    }


def halves(values):
    high = values.astype(jnp.bfloat16)
    return high, (values - high.astype(jnp.float32)).astype(jnp.bfloat16)


def dot(left, right):
    return lax.dot_general(
        left, right, (((1,), (0,)), ((), ())), preferred_element_type=jnp.float32
    )


def dot_right(values, table):
    high, low = halves(values)
    return dot(high, table[0]) + (dot(high, table[1]) + dot(low, table[0]))


def dot_left(table, values):
    high, low = halves(values)
    return dot(table, jnp.concatenate((high, low, high), axis=0))


def turn_lanes(real, imag, cosine, mixed, sign):
    common = dot_right(real + imag, cosine)
    if sign > 0:
        return common - dot_right(imag, mixed.at[1]), common + dot_right(real, mixed.at[0])
    return common + dot_right(imag, mixed.at[0]), common - dot_right(real, mixed.at[1])


def half_lengths(even, odd):
    return even + odd, even - odd


def dot_receive(table, found):
    first, second = half_lengths(*(dot_left(table[one], found[one]) for one in range(2)))
    mid = first.shape[0] // 2
    return (
        jnp.concatenate((first[:mid], second[:mid]), axis=0),
        jnp.concatenate((first[mid:], second[mid:]), axis=0),
    )


def dot_mirror(table, values):
    high, low = halves(values)
    low_rest = (values - high.astype(jnp.float32) - low.astype(jnp.float32)).astype(jnp.bfloat16)
    return dot(table, high) + (dot(table, low) + dot(table, low_rest))


def merge_tails(first, second):
    return first + pltpu.roll(second, 64, 1)


def to_half_kernel(field, cosine, mixed, send, out, turned):
    pair, length = field.shape[3], field.shape[4]
    members, rows = out.shape[0], out.shape[-2]
    mid = members // 2
    out = out.at[:, 0, 0] if len(out.shape) == 6 else out.at[:, 0]
    parts = [field[0, 0, part].reshape(pair * length, length) for part in range(2)]
    parts = turn_lanes(*parts, cosine, mixed, 1)
    for part in range(2):
        turned[part, 0] = parts[part][:, :128]
        turned[part, 1] = parts[part][:, 128:]
    tails = []
    for one in range(pair):
        found = []
        for parity in range(2):
            rows_of = pl.ds(one * length + parity, length // 2, stride=2)
            found.append(
                jnp.concatenate(
                    [
                        jnp.concatenate((turned[part, 0, rows_of], turned[part, 1, rows_of]), axis=1)
                        for part in range(2)
                    ],
                    axis=0,
                )
            )
        done = half_lengths(*(dot_left(send[parity], found[parity]) for parity in range(2)))
        for half in range(2):
            to = slice(half * mid, (half + 1) * mid)
            out[to, one] = done[half][:, :128].reshape(mid, rows, 128)
        tails.append([piece[:, 128:] for piece in done])
    for half in range(2):
        to = slice(half * mid, (half + 1) * mid)
        out[to, 2] = merge_tails(tails[0][half], tails[1][half]).reshape(mid, rows, 128)


def received(ref, start, stride, count):
    return ref[pl.ds(start, count, stride=stride), :]


def plane(got, start, stride, place, slab, with_main, with_tail):
    count = got.shape[0] // stride
    found = [[], []]
    for part in range(2):
        row = start + part * slab + place
        mains, tails = [None, None], [None, None]
        if with_main:
            mains = [received(got, one * 2 * slab + row, stride, count) for one in range(2)]
            row = row + 4 * slab
        if with_tail:
            tail = received(got, row, stride, count)
            tails = [tail, pltpu.roll(tail, 64, 1)]
        for one in range(2):
            pieces = [piece for piece in (mains[one], tails[one]) if piece is not None]
            found[one].append(jnp.concatenate(pieces, axis=1) if len(pieces) > 1 else pieces[0])
    return [jnp.concatenate(one, axis=0) for one in found]


def to_space_kernel(slab, start, stride, got, receive, space):
    length = space.shape[2]
    for one in range(2):
        place = 2 * pl.program_id(0) + one
        values = plane(got, start, stride, place, slab, True, True)
        real, imag = dot_receive(receive, values)
        space[one, :length] = real[:, :length]
        space[one, length:] = imag[:, :length]


def folded(values):
    return values.reshape(-1, 8, values.shape[-1]).sum(axis=0)


def apply_kernel(
    slab, start, stride, band, weights, got, spaces, potential, perturbation, before,
    receive, cosine, mixed, send, out_main, out_tail, inner, density
):
    length = potential.shape[1]
    members, rows = out_main.shape[0], out_main.shape[3]
    step = pl.program_id(0)
    twice_weight = 2.0 * weights[0]

    @pl.when(step == 0)
    def _():
        inner[...] = jnp.zeros_like(inner)

    tails = []
    sums = []
    for one in range(2):
        values = plane(got, start, stride, 2 * step + one, slab, True, True)
        real, imag = (piece[:, :length] for piece in dot_receive(receive, values))
        own_real, own_imag = spaces[band, one, :length], spaces[band, one, length:]
        local = twice_weight * (own_real * real + own_imag * imag)
        if before is not None:
            local = local + before[one]
        sums.append(local)
        field, change = potential[one], perturbation[one]
        real = field * real + change * own_real
        imag = field * imag + change * own_imag
        for other in range(2):
            left_real, left_imag = spaces[other, one, :length], spaces[other, one, length:]
            inner[0, other] += folded(left_real * real + left_imag * imag)
            inner[1, other] += folded(left_real * imag - left_imag * real)
        turned = jnp.concatenate(turn_lanes(real, imag, cosine, mixed, -1), axis=0)
        done = dot_left(send[...], turned)
        out_main[:, 0, one] = done[:, :128].reshape(members, rows, 128)
        tails.append(done[:, 128:])
    tail = merge_tails(*tails).reshape(members, rows, 128)
    if out_tail is None:
        out_main[:, 0, 2] = tail
    else:
        out_tail[:, 0] = tail
    for one in range(2):
        density[one] = sums[one]


def lanes_from(*pieces):
    lane = lax.broadcasted_iota(jnp.int32, pieces[0][0].shape, 1)
    width = 128 // len(pieces)
    moved = [pltpu.roll(values, by, 1) if by else values for values, by in pieces]
    made = moved[-1]
    for place in range(len(pieces) - 2, -1, -1):
        made = jnp.where(lane < (place + 1) * width, moved[place], made)
    return made


def pack(planes, pair, alone, out):
    members = out.shape[0]
    tails = []
    for first in range(0, 12, 4):
        one, two, three, four = (planes(first + by) for by in range(4))
        mains = (lanes_from((one, 0), (two, 64)), lanes_from((three, 0), (four, 64)))
        tails.append(lanes_from((one, 64), (two, 96), (three, 0), (four, 32)))
        out[:, 6 * first : 6 * first + 24] = dot_mirror(
            pair[...], jnp.concatenate(mains, axis=0)
        ).reshape(members, 24, 128)
    out[:, 72:96] = dot_mirror(pair[...], jnp.concatenate(tails[:2], axis=0)).reshape(
        members, 24, 128
    )
    out[:, 96:112] = dot_mirror(alone[...], tails[2]).reshape(members, 16, 128)


def unpack(got, place):
    members = got.shape[0] // 112
    found = []
    for quad in range(3):
        one = received(got, 24 * quad + place, 112, members)
        two = received(got, 24 * quad + 12 + place, 112, members)
        tail = received(got, 72 + 12 * quad + place, 112, members)
        found += [
            lanes_from((one, 0), (tail, 64)),
            lanes_from((one, 64), (tail, 32)),
            lanes_from((two, 0), (tail, 0)),
            lanes_from((two, 64), (tail, 96)),
        ]
    return jnp.concatenate(found, axis=0)


def pack_kernel(pool, density, pair, alone, kept, given):
    length = density.shape[1]
    own = pool[0] == 0

    def halves_of(place):
        main = density[place, :, :128]
        tail = jnp.concatenate(
            (density[place, :, 128:], jnp.zeros((length, 64), jnp.float32)), axis=1
        )
        return lanes_from((main, 0), (tail, 64)), lanes_from((main, 64), (tail, 32))

    def one_half(which):
        def planes(place):
            low, high = halves_of(place)
            return jnp.where(own, low, high) if which else jnp.where(own, high, low)

        return planes

    pack(one_half(True), pair, alone, kept)
    pack(one_half(False), pair, alone, given)


def frequencies(length, first, lanes, first_lane):
    rows = lax.broadcasted_iota(jnp.int32, (length, lanes), 0)
    columns = lax.broadcasted_iota(jnp.int32, (length, lanes), 1) + first_lane
    row = jnp.where(rows < length // 2, rows, rows - length).astype(jnp.float32)
    column = jnp.where(columns < length // 2, columns, columns - length).astype(jnp.float32)
    outer = jnp.where(first < length // 2, first, first - length).astype(jnp.float32)
    return 0.5 * RECIPROCAL_SQUARE * (outer * outer + row * row + column * column)


def inner_kernel(slab, me, energies, orbitals, responses, inner):
    length = orbitals.shape[4]
    step = pl.program_id(0)

    @pl.when(step == 0)
    def _():
        inner[...] = jnp.zeros_like(inner)

    for one in range(2):
        kinetic = frequencies(length, me[0] * slab + 2 * step + one, length, 0)
        for band in range(2):
            shifted = kinetic - energies[0, band]
            real = shifted * responses[0, band, 0, one]
            imag = shifted * responses[0, band, 1, one]
            for other in range(2):
                left_real, left_imag = orbitals[0, other, 0, one], orbitals[0, other, 1, one]
                inner[0, other, band] += folded(left_real * real + left_imag * imag)
                inner[1, other, band] += folded(left_real * imag - left_imag * real)


def direct_kernel(slab, me, energies, inner, orbitals, responses, out):
    length = orbitals.shape[4]
    cells = float(length**3)
    for one in range(2):
        kinetic = frequencies(length, me[0] * slab + 2 * pl.program_id(0) + one, length, 0)
        inverse = 1.0 / (1.0 + kinetic)
        for band in range(2):
            shifted = kinetic - energies[0, band]
            real = shifted * responses[0, band, 0, one]
            imag = shifted * responses[0, band, 1, one]
            for other in range(2):
                left_real, left_imag = orbitals[0, other, 0, one], orbitals[0, other, 1, one]
                by_real = inner[0, other, band] / cells
                by_imag = inner[1, other, band] / cells
                real = real - (left_real * by_real - left_imag * by_imag)
                imag = imag - (left_real * by_imag + left_imag * by_real)
            out[0, band, 0, one] = responses[0, band, 0, one] - real * inverse
            out[0, band, 1, one] = responses[0, band, 1, one] - imag * inverse


def finish_kernel(slab, start, stride, tail, me, got, receive, base, out):
    length = base.shape[4]
    for one in range(2):
        place = 2 * pl.program_id(0) + one
        values = plane(got, start, stride, place, slab, not tail, tail)
        applied = dot_receive(receive, values)
        kinetic = frequencies(length, me[0] * slab + place, 128, 128 if tail else 0)
        inverse = 1.0 / (1.0 + kinetic)
        for part in range(2):
            out[0, 0, part, one] = base[0, 0, part, one] - applied[part] * inverse


def mirror_kernel(got, single, pair, alone, out, natural, loose):
    for place in range(12):
        loose[place] = unpack(got, place)
        natural[place] = dot_mirror(single[...], loose[place])
    pack(lambda place: loose[place], pair, alone, out)


def swap_kernel(got, order, natural, out):
    for place in range(12):
        out[place] = (natural[place] + dot_mirror(order[...], unpack(got, place))) * 0.125


def cost(flops, moved):
    return pl.CostEstimate(flops=int(flops), bytes_accessed=int(moved), transcendentals=0)


def whole():
    return pl.BlockSpec(memory_space=pltpu.VMEM)


def scalars():
    return pl.BlockSpec(memory_space=pltpu.SMEM)


def call(kernel, name, grid, ins, outs, shapes, estimate, aliases=None, scratch=()):
    return pl.pallas_call(
        kernel,
        grid=(grid,),
        in_specs=ins,
        out_specs=outs,
        out_shape=shapes,
        compiler_params=pltpu.CompilerParams(
            dimension_semantics=("arbitrary",), vmem_limit_bytes=VMEM_BYTES
        ),
        cost_estimate=estimate,
        input_output_aliases=aliases or {},
        scratch_shapes=scratch,
        name=name,
    )


def f32(*shape):
    return jax.ShapeDtypeStruct(shape, jnp.float32)


def packed_body(orbitals, responses, energies, weights, potential, perturbation):
    length = orbitals.shape[-1]
    slab = orbitals.shape[3]
    members = length // slab
    pairs = slab // 2
    rows = 2 * slab
    table = {key: jnp.asarray(value) for key, value in matrices(length, slab, members).items()}
    me = lax.axis_index("pw").astype(jnp.int32).reshape(1)
    pool = lax.axis_index("pool").astype(jnp.int32).reshape(1)
    field_bytes = 4 * members * pairs * 3 * rows * 128
    stage_flops = 6 * 2 * 2 * length * length * length * slab * 2

    half_spec = pl.BlockSpec((members, 1, 3, rows, 128), lambda p: (0, p, 0, 0, 0))
    half_shape = f32(members, pairs, 3, rows, 128)

    def exchange(values, after=None):
        values = values.reshape(members, -1, 128)
        if after is not None:
            values, _ = lax.optimization_barrier((values, after))
        return lax.all_to_all(values, "pw", split_axis=0, concat_axis=0, tiled=True)

    def to_half(field, band, into=None, slot=None):
        def kernel(field, cosine, mixed, send, *rest):
            to_half_kernel(field, cosine, mixed, send, *rest[-2:])

        spec, shape = half_spec, half_shape
        if slot is not None:
            spec = pl.BlockSpec((members, 1, 1, 3, rows, 128), lambda p: (0, p, slot, 0, 0, 0))
            shape = f32(members, pairs, 2, 3, rows, 128)
        return call(
            kernel,
            "to_half",
            pairs,
            [
                pl.BlockSpec((1, 1, 2, 2, length, length), lambda p: (0, band, 0, p, 0, 0)),
                whole(),
                whole(),
                whole(),
            ]
            + ([] if into is None else [pl.BlockSpec(memory_space=pl.ANY)]),
            spec,
            shape,
            cost(2 * stage_flops, 2 * field_bytes),
            {} if into is None else {4: 0},
            [pltpu.VMEM((2, 2, 2 * length, 128), jnp.float32)],
        )(
            field, table["cosine"], table["mixed"], table["inverse_send"],
            *(() if into is None else (into,)),
        )

    def to_space(got, start, stride):
        return call(
            functools.partial(to_space_kernel, slab, start, stride),
            "to_space",
            pairs,
            [whole(), whole()],
            pl.BlockSpec((2, 2 * length, length), lambda p: (p, 0, 0)),
            f32(slab, 2 * length, length),
            cost(stage_flops, 2 * field_bytes),
        )(got.reshape(-1, 128), table["inverse_receive"])

    plane_spec = pl.BlockSpec((2, length, length), lambda p: (p, 0, 0))
    send_specs = [
        pl.BlockSpec((members, 1, 2, rows, 128), lambda p: (0, p, 0, 0, 0)),
        pl.BlockSpec((members, 1, rows, 128), lambda p: (0, p, 0, 0)),
    ]
    send_shapes = [
        f32(members, pairs, 2, rows, 128),
        f32(members, pairs, rows, 128),
    ]
    block_shape = f32(members, 112, 128)
    inner_spec = pl.BlockSpec((2, 2, 8, length), lambda p: (0, 0, 0, 0))

    def apply_first(got, spaces, field, change):
        def kernel(weights, got, first, second, field, change, *tables_and_outs):
            receive, cosine, mixed, send, main, inner, density = tables_and_outs
            apply_kernel(
                slab, 3 * rows, 6 * rows, 0, weights, got, Both(first, second), field, change, None,
                receive, cosine, mixed, send, main, None, inner, density,
            )

        return call(
            kernel,
            "apply_first",
            pairs,
            [scalars(), whole(), space_spec, space_spec, plane_spec, plane_spec] + [whole()] * 4,
            [half_spec, inner_spec, plane_spec],
            [half_shape, f32(2, 2, 8, length), f32(slab, length, length)],
            cost(3 * stage_flops, 5 * field_bytes),
        )(
            weights, got.reshape(-1, 128), *spaces, field, change,
            table["inverse_receive"], table["cosine"], table["mixed"], table["forward_send"],
        )

    def apply_last(got, spaces, field, change, before):
        def kernel(weights, got, first, second, field, change, before, *tables_and_outs):
            receive, cosine, mixed, send, main, tail, inner, density = tables_and_outs
            apply_kernel(
                slab, 0, 3 * rows, 1, weights, got, Both(first, second), field, change, before,
                receive, cosine, mixed, send, main, tail, inner, density,
            )

        return call(
            kernel,
            "apply_last",
            pairs,
            [scalars(), whole(), space_spec, space_spec] + [plane_spec] * 3 + [whole()] * 4,
            send_specs + [inner_spec, plane_spec],
            send_shapes + [f32(2, 2, 8, length), f32(slab, length, length)],
            cost(3 * stage_flops, 5 * field_bytes),
        )(
            weights, got.reshape(-1, 128), *spaces, field, change, before,
            table["inverse_receive"], table["cosine"], table["mixed"], table["forward_send"],
        )

    space_spec = pl.BlockSpec((2, 2 * length, length), lambda p: (p, 0, 0))
    bands_spec = pl.BlockSpec((1, 2, 2, 2, length, length), lambda p: (0, 0, 0, p, 0, 0))

    def finish(base, got, band, start, stride, tail):
        lane_block = 1 if tail else 0
        one_spec = pl.BlockSpec(
            (1, 1, 2, 2, length, 128), lambda p: (0, band, 0, p, 0, lane_block)
        )
        return call(
            functools.partial(finish_kernel, slab, start, stride, tail),
            "finish",
            pairs,
            [scalars(), whole(), whole(), one_spec],
            one_spec,
            f32(*base.shape),
            cost(stage_flops, 2 * field_bytes),
            {3: 0},
        )(me, got.reshape(-1, 128), table["forward_receive"], base)

    field = jnp.transpose(potential, (1, 0, 2))
    change = jnp.transpose(perturbation, (1, 0, 2))
    got_one = exchange(to_half(orbitals, 0))
    half_two = to_half(orbitals, 1, None, 0)
    got_two = exchange(to_half(responses, 0, half_two, 1), got_one)
    direct_inner = call(
        functools.partial(inner_kernel, slab),
        "inner",
        pairs,
        [scalars(), scalars(), bands_spec, bands_spec],
        pl.BlockSpec((2, 2, 2, 8, length), lambda p: (0, 0, 0, 0, 0)),
        f32(2, 2, 2, 8, length),
        cost(32 * field_bytes, 4 * field_bytes),
    )(me, energies, orbitals, responses)
    got_last = exchange(to_half(responses, 1), (got_two, direct_inner))
    spaces = [to_space(got_one, 0, 3 * rows), to_space(got_two, 0, 6 * rows)]
    send_first, inner_first, before = apply_first(got_two, spaces, field, change)
    back_first = exchange(send_first, got_last)
    last_main, last_tail, inner_last, density = apply_last(
        got_last, spaces, field, change, before
    )
    kept, given = call(
        pack_kernel,
        "pack",
        1,
        [scalars(), whole(), whole(), whole()],
        [whole(), whole()],
        [block_shape, block_shape],
        cost(4e9, 5e6),
    )(pool, density, table["pair"], table["alone"])
    swap = [(0, 1), (1, 0)]
    local_inner = direct_inner + jnp.stack((inner_first, inner_last), axis=2)
    riding = jnp.sum(local_inner, axis=(3, 4)).reshape(1, 1, 8)
    riding = jnp.pad(riding, ((0, 0), (0, 0), (0, 120)))
    row = lax.broadcasted_iota(jnp.int32, block_shape.shape, 1)
    summed = jnp.where(row < 108, kept + lax.ppermute(given, "pool", swap), riding)
    got_density = exchange(summed, back_first)
    inner = jnp.sum(got_density[:, 108, :8], axis=0).reshape(2, 2, 2)
    back_tail = exchange(last_tail, got_density)
    base = call(
        functools.partial(direct_kernel, slab),
        "direct",
        pairs,
        [scalars(), scalars(), scalars(), bands_spec, bands_spec],
        bands_spec,
        f32(*responses.shape),
        cost(32 * field_bytes, 6 * field_bytes),
    )(me, energies, inner, orbitals, responses)
    mirrored, natural = call(
        mirror_kernel,
        "mirror",
        1,
        [whole()] * 4,
        [whole(), whole()],
        [block_shape, f32(slab, length, 128)],
        cost(4e9, 4e6),
        scratch=[pltpu.VMEM((slab, length, 128), jnp.float32)],
    )(got_density.reshape(-1, 128), table["loose_mirror"], table["loose_pair"], table["loose_alone"])
    got_mirrored = exchange(mirrored, (back_tail, base))
    base = finish(base, back_first, 0, 0, 3 * rows, False)
    base = finish(base, back_first, 0, 2 * rows, 3 * rows, True)
    back_main = exchange(last_main, (got_mirrored, base))
    symmetric = call(
        swap_kernel,
        "swap",
        1,
        [whole()] * 3,
        whole(),
        f32(slab, length, 128),
        cost(1e9, 4e6),
    )(got_mirrored.reshape(-1, 128), table["loose_order"], natural)
    other = lax.ppermute(symmetric, "pool", swap)
    low = jnp.where(pool == 0, symmetric, other)
    high = jnp.where(pool == 0, other, symmetric)
    response_density = jnp.concatenate(
        (low[..., :64], high[..., :64], low[..., 64:96], high[..., 64:96]), axis=2
    )
    base = finish(base, back_tail, 1, 0, rows, True)
    base, response_density, back_main = lax.optimization_barrier(
        (base, response_density, back_main)
    )
    base = finish(base, back_main, 1, 0, 2 * rows, False)
    return base, response_density


class Both:
    def __init__(self, *refs):
        self.refs = refs

    def __getitem__(self, index):
        return self.refs[index[0]][index[1:]]


def tables(length):
    indices = jnp.arange(length, dtype=jnp.int32)
    angles = (indices[:, None] * indices[None, :] % length).astype(jnp.float32) * (
        2.0 * math.pi / length
    )
    factor = 1.0 / math.sqrt(length)
    return (jnp.cos(angles) * factor, jnp.sin(angles) * factor)


def apply_table(values, table_in, along_axis):
    rotated = jnp.tensordot(
        values, table_in, axes=((along_axis,), (0,)), precision=lax.Precision.HIGHEST
    )
    return jnp.moveaxis(rotated, -1, along_axis)


def transform(field_in, along_axis, cosine_table, sine_table, phase_sign):
    real_part = field_in[:, :, 0]
    imag_part = field_in[:, :, 1]
    real_cos = apply_table(real_part, cosine_table, along_axis)
    real_sin = apply_table(real_part, sine_table, along_axis)
    imag_cos = apply_table(imag_part, cosine_table, along_axis)
    imag_sin = apply_table(imag_part, sine_table, along_axis)
    return jnp.stack((real_cos - phase_sign * imag_sin, phase_sign * real_sin + imag_cos), axis=2)


def signed_freq(indices, length):
    return jnp.where(indices < length // 2, indices, indices - length).astype(jnp.float32)


def negated(values, along_axis):
    return jnp.roll(jnp.flip(values, along_axis), 1, along_axis)


def products(left_side, right_side):
    band_count = left_side.shape[0]
    highest = lax.Precision.HIGHEST
    left_real = left_side[:, 0].reshape(band_count, -1)
    left_imag = left_side[:, 1].reshape(band_count, -1)
    right_real = right_side[:, 0].reshape(band_count, -1)
    right_imag = right_side[:, 1].reshape(band_count, -1)
    real_sum = jnp.dot(left_real, right_real.T, precision=highest) + jnp.dot(
        left_imag, right_imag.T, precision=highest
    )
    imag_sum = jnp.dot(left_real, right_imag.T, precision=highest) - jnp.dot(
        left_imag, right_real.T, precision=highest
    )
    return (real_sum, imag_sum)


def plain_body(orbitals, responses, energies, weights, potential, perturbation):
    length = orbitals.shape[-1]
    slab_rows = orbitals.shape[3]
    cosine_table, sine_table = tables(length)

    def to_space(field_in):
        return transform(
            transform(field_in, 4, cosine_table, sine_table, 1.0), 3, cosine_table, sine_table, 1.0
        )

    def finish_one(one_piece):
        return transform(one_piece, 2, cosine_table, sine_table, 1.0)

    orbital_space = finish_one(
        lax.all_to_all(to_space(orbitals), "pw", split_axis=4, concat_axis=3, tiled=True)
    )
    response_space = finish_one(
        lax.all_to_all(to_space(responses), "pw", split_axis=4, concat_axis=3, tiled=True)
    )
    partial_value = (
        2.0
        * weights[0]
        * jnp.sum(
            orbital_space[0, :, 0] * response_space[0, :, 0]
            + orbital_space[0, :, 1] * response_space[0, :, 1],
            axis=0,
        )
    )
    applied_space = potential * response_space + perturbation * orbital_space
    first_row = lax.axis_index("pw") * slab_rows
    row_freq = signed_freq(first_row + jnp.arange(slab_rows, dtype=jnp.int32), length)
    full_freq = signed_freq(jnp.arange(length, dtype=jnp.int32), length)
    kinetic = (
        0.5
        * RECIPROCAL_SQUARE
        * (
            row_freq[:, None, None] * row_freq[:, None, None]
            + full_freq[None, :, None] * full_freq[None, :, None]
            + full_freq[None, None, :] * full_freq[None, None, :]
        )
    )
    shifted = kinetic[None] - energies[0][:, None, None, None]
    direct = shifted[None, :, None] * responses
    sectioned = transform(
        transform(applied_space, 4, cosine_table, sine_table, -1.0),
        2,
        cosine_table,
        sine_table,
        -1.0,
    )
    residual = direct + transform(
        lax.all_to_all(sectioned, "pw", split_axis=3, concat_axis=4, tiled=True),
        3,
        cosine_table,
        sine_table,
        -1.0,
    )
    over_real, over_imag = lax.psum(products(orbitals[0], residual[0]), "pw")
    highest = lax.Precision.HIGHEST
    orbital_real = orbitals[0, :, 0]
    orbital_imag = orbitals[0, :, 1]
    combine_real = jnp.einsum(
        "mn,mxyz->nxyz", over_real, orbital_real, precision=highest
    ) - jnp.einsum("mn,mxyz->nxyz", over_imag, orbital_imag, precision=highest)
    combine_imag = jnp.einsum(
        "mn,mxyz->nxyz", over_imag, orbital_real, precision=highest
    ) + jnp.einsum("mn,mxyz->nxyz", over_real, orbital_imag, precision=highest)
    cell_count = float(length**3)
    projected = residual - jnp.stack((combine_real, combine_imag), axis=1)[None] / cell_count
    new_responses = responses - projected / (1.0 + kinetic)[None, None, None]
    summed = lax.psum(partial_value, "pool")
    mirrored = summed + negated(summed, 0)
    row_slab = lax.all_to_all(mirrored, "pw", split_axis=0, concat_axis=1, tiled=True)
    signsum = row_slab + negated(row_slab, 1)
    swapped = lax.all_to_all(signsum, "pw", split_axis=1, concat_axis=0, tiled=True)
    total_sym = signsum + jnp.transpose(swapped, (1, 0, 2))
    return (new_responses, total_sym / 8.0)


def body(orbitals, responses, energies, weights, potential, perturbation):
    slab, length = orbitals.shape[3], orbitals.shape[-1]
    fits = slab == 12 and length == 192 and orbitals.shape[0] == 1 and orbitals.shape[1] == 2
    return (packed_body if fits else plain_body)(
        orbitals, responses, energies, weights, potential, perturbation
    )


def solution(mesh):
    placed = (
        P("pool", None, None, "pw", None, None),
        P("pool", None, None, "pw", None, None),
        P("pool", None),
        P("pool"),
        P(None, "pw", None),
        P(None, "pw", None),
    )
    return jax.shard_map(
        body,
        mesh=mesh,
        in_specs=placed,
        out_specs=(P("pool", None, None, "pw", None, None), P("pw", None, None)),
        check_vma=False,
    )
```

```python
import functools
import math

import jax
import jax.numpy as jnp
import ml_dtypes
import numpy as np
from jax import lax
from jax.experimental import pallas as pl
from jax.experimental.pallas import tpu as pltpu
from jax.sharding import PartitionSpec as P

RECIPROCAL_SQUARE = 0.023428
VMEM_BYTES = 63 * 1024 * 1024


def split_table(table):
    high = table.astype(ml_dtypes.bfloat16)
    low = (table - high.astype(np.float64)).astype(ml_dtypes.bfloat16)
    return np.stack((high, low))


def long_table(table):
    high, low = split_table(table)
    return np.concatenate((high, high, low), axis=1)


@functools.cache
def matrices(length, slab, members):
    index = np.arange(length)
    angles = (index[:, None] * index[None, :] % length) * (2.0 * math.pi / length)
    cosine = np.cos(angles) / math.sqrt(length)
    sine = np.sin(angles) / math.sqrt(length)
    lanes = 128 * -(-length // 128)
    pad = ((0, 0), (0, lanes - length))
    inverse = np.block([[cosine, -sine], [sine, cosine]])
    forward = np.block([[cosine, sine], [-sine, cosine]])
    sent = np.arange(2 * length).reshape(2, members, slab).transpose(1, 0, 2).reshape(-1)
    got = np.arange(2 * length).reshape(2, members, slab // 4, 2, 2).transpose(4, 0, 3, 1, 2)
    got = got.reshape(2, -1)
    first = np.arange(2 * length).reshape(2, 2, length // 2)[:, 0].reshape(-1)
    parity = np.arange(2 * length).reshape(length, 2).T
    mirror = np.eye(length) + np.eye(length)[(-index) % length]
    both = np.zeros((members, 2, slab, 2, length))
    for which in range(2):
        both[:, which, :, which, :] = mirror.reshape(members, slab, length)
    both = both.reshape(2 * length, 2, length)
    alone = np.pad(mirror.reshape(members, slab, length), ((0, 0), (0, 4), (0, 0)))
    alone = alone.reshape(-1, length)
    loose = index.reshape(members, slab).T.reshape(-1)
    fold = np.minimum(index, length - index)
    swapped = np.zeros((2, length, slab + 1, members))
    swapped[0, index, fold % slab, fold // slab] = 1.0
    swapped[0, length // 2] = 0.0
    swapped[0, length // 2, slab, members // 2] = 1.0
    folded = (length - fold) % length
    swapped[1, index, folded % slab, folded // slab] = 1.0
    swapped[1, 0] = 0.0
    swapped[1, 0, slab, 0] = 1.0
    return {
        "cosine": split_table(np.pad(cosine, pad)),
        "mixed": np.stack(
            [split_table(np.pad(sine + sign * cosine, pad)) for sign in (-1.0, 1.0)]
        ),
        "inverse_send": np.stack([long_table(inverse[sent[:length]][:, one]) for one in parity]),
        "inverse_receive": np.stack([long_table(inverse[first][:, one]) for one in got]),
        "forward_send": long_table(forward[sent]),
        "forward_receive": np.stack([long_table(forward[first][:, one]) for one in got]),
        "pair": both.reshape(2 * length, -1).astype(ml_dtypes.bfloat16),
        "alone": alone.astype(ml_dtypes.bfloat16),
        "loose_pair": both[:, :, loose].reshape(2 * length, -1).astype(ml_dtypes.bfloat16),
        "loose_alone": alone[:, loose].astype(ml_dtypes.bfloat16),
        "loose_mirror": mirror[:, loose].astype(ml_dtypes.bfloat16),
        "swapped": swapped.reshape(2 * length, -1).astype(ml_dtypes.bfloat16),
    }


def halves(values):
    high = values.astype(jnp.bfloat16)
    return high, (values - high.astype(jnp.float32)).astype(jnp.bfloat16)


def dot(left, right):
    return lax.dot_general(
        left, right, (((1,), (0,)), ((), ())), preferred_element_type=jnp.float32
    )


def dot_right(values, table):
    high, low = halves(values)
    return dot(high, table[0]) + (dot(high, table[1]) + dot(low, table[0]))


def dot_left(table, values):
    high, low = halves(values)
    return dot(table, jnp.concatenate((high, low, high), axis=0))


def turn_lanes(real, imag, cosine, mixed, sign):
    common = dot_right(real + imag, cosine)
    if sign > 0:
        return common - dot_right(imag, mixed.at[1]), common + dot_right(real, mixed.at[0])
    return common + dot_right(imag, mixed.at[0]), common - dot_right(real, mixed.at[1])


def half_lengths(even, odd):
    return even + odd, even - odd


def dot_receive(table, found):
    first, second = half_lengths(*(dot_left(table[one], found[one]) for one in range(2)))
    mid = first.shape[0] // 2
    return (
        jnp.concatenate((first[:mid], second[:mid]), axis=0),
        jnp.concatenate((first[mid:], second[mid:]), axis=0),
    )


def dot_mirror(table, values):
    high, low = halves(values)
    low_rest = (values - high.astype(jnp.float32) - low.astype(jnp.float32)).astype(jnp.bfloat16)
    return dot(table, high) + (dot(table, low) + dot(table, low_rest))


def merge_tails(first, second):
    return first + pltpu.roll(second, 64, 1)


def to_half_kernel(field, cosine, mixed, send, out, turned):
    pair, length = field.shape[3], field.shape[4]
    members, rows = out.shape[0], out.shape[-2]
    mid = members // 2
    out = out.at[:, 0, 0]
    parts = [field[0, 0, part].reshape(pair * length, length) for part in range(2)]
    parts = turn_lanes(*parts, cosine, mixed, 1)
    for part in range(2):
        turned[part, 0] = parts[part][:, :128]
        turned[part, 1] = parts[part][:, 128:]
    tails = []
    for one in range(pair):
        found = []
        for parity in range(2):
            rows_of = pl.ds(one * length + parity, length // 2, stride=2)
            found.append(
                jnp.concatenate(
                    [
                        jnp.concatenate((turned[part, 0, rows_of], turned[part, 1, rows_of]), axis=1)
                        for part in range(2)
                    ],
                    axis=0,
                )
            )
        done = half_lengths(*(dot_left(send[parity], found[parity]) for parity in range(2)))
        for half in range(2):
            to = slice(half * mid, (half + 1) * mid)
            out[to, one] = done[half][:, :128].reshape(mid, rows, 128)
        tails.append([piece[:, 128:] for piece in done])
    for half in range(2):
        to = slice(half * mid, (half + 1) * mid)
        out[to, 2] = merge_tails(tails[0][half], tails[1][half]).reshape(mid, rows, 128)


def received(ref, start, stride, count):
    return ref[pl.ds(start, count, stride=stride), :]


def plane(parts_of, place, slab, with_main, with_tail):
    def rows_at(row):
        pieces = [
            received(ref, start + row, stride, ref.shape[0] // stride)
            for ref, start, stride in parts_of
        ]
        return jnp.concatenate(pieces, axis=0)

    found = [[], []]
    for part in range(2):
        row = part * slab + place
        mains, tails = [None, None], [None, None]
        if with_main:
            mains = [rows_at(one * 2 * slab + row) for one in range(2)]
            row = row + 4 * slab
        if with_tail:
            tail = rows_at(row)
            tails = [tail, pltpu.roll(tail, 64, 1)]
        for one in range(2):
            pieces = [piece for piece in (mains[one], tails[one]) if piece is not None]
            found[one].append(jnp.concatenate(pieces, axis=1) if len(pieces) > 1 else pieces[0])
    return [jnp.concatenate(one, axis=0) for one in found]


def to_space_kernel(slab, starts, strides, *refs):
    *gots, receive, space = refs
    length = space.shape[2]
    parts_of = list(zip(gots if len(gots) > 1 else gots * 2, starts, strides))
    for one in range(2):
        place = 2 * pl.program_id(0) + one
        values = plane(parts_of, place, slab, True, True)
        real, imag = dot_receive(receive, values)
        space[one, :length] = real[:, :length]
        space[one, length:] = imag[:, :length]


def folded(values):
    return values.reshape(-1, 8, values.shape[-1]).sum(axis=0)


def apply_kernel(
    slab, starts, stride, band, weights, got, spaces, potential, perturbation, before,
    receive, cosine, mixed, send, out_main, out_tail, inner, density
):
    length = potential.shape[1]
    members, rows = out_main.shape[0], out_main.shape[3]
    step = pl.program_id(0)
    twice_weight = 2.0 * weights[0]

    @pl.when(step == 0)
    def _():
        inner[...] = jnp.zeros_like(inner)

    tails = []
    sums = []
    for one in range(2):
        parts_of = [(got, start, stride) for start in starts]
        values = plane(parts_of, 2 * step + one, slab, True, True)
        real, imag = (piece[:, :length] for piece in dot_receive(receive, values))
        own_real, own_imag = spaces[band, one, :length], spaces[band, one, length:]
        local = twice_weight * (own_real * real + own_imag * imag)
        if before is not None:
            local = local + before[one]
        sums.append(local)
        field, change = potential[one], perturbation[one]
        real = field * real + change * own_real
        imag = field * imag + change * own_imag
        for other in range(2):
            left_real, left_imag = spaces[other, one, :length], spaces[other, one, length:]
            inner[0, other] += folded(left_real * real + left_imag * imag)
            inner[1, other] += folded(left_real * imag - left_imag * real)
        turned = jnp.concatenate(turn_lanes(real, imag, cosine, mixed, -1), axis=0)
        done = dot_left(send[...], turned)
        out_main[:, 0, one] = done[:, :128].reshape(members, rows, 128)
        tails.append(done[:, 128:])
    tail = merge_tails(*tails).reshape(members, rows, 128)
    if out_tail is None:
        out_main[:, 0, 2] = tail
    else:
        out_tail[:, 0] = tail
    for one in range(2):
        density[one] = sums[one]


def lanes_of(values):
    return lax.broadcasted_iota(jnp.int32, values.shape, 1)


def moved(values, by):
    return pltpu.roll(values, by % 128, 1) if by % 128 else values


def pack(planes, count, width, pair, alone, out):
    members = out.shape[0]
    blocks = []
    for block in range(-(-count * width // 128)):
        made = None
        for place in range(count):
            start = place * width - 128 * block
            if start >= 128 or start + width <= 0:
                continue
            values = moved(planes(place), start)
            made = values if made is None else jnp.where(lanes_of(values) < start, made, values)
        blocks.append(made)
    for first in range(0, len(blocks) - 1, 2):
        out[:, 12 * first : 12 * first + 24] = dot_mirror(
            pair[...], jnp.concatenate(blocks[first : first + 2], axis=0)
        ).reshape(members, 24, 128)
    out[:, 12 * len(blocks) - 12 :] = dot_mirror(alone[...], blocks[-1]).reshape(members, 16, 128)


def unpack(got, place, count, width, rows):
    members = got.shape[0] // rows
    blocks = [
        received(got, 12 * block + place, rows, members)
        for block in range(-(-count * width // 128))
    ]
    found = []
    for one in range(count):
        block, start = divmod(one * width, 128)
        values = moved(blocks[block], -start)
        if start + width > 128:
            rest = moved(blocks[block + 1], -start)
            values = jnp.where(lanes_of(values) < 128 - start, values, rest)
        found.append(values)
    return jnp.concatenate(found, axis=0)


def pack_kernel(pool, density, pair, alone, kept, given):
    length = density.shape[1]
    own = pool[0] == 0

    def one_half(which):
        def planes(place):
            low = density[place, :, :128]
            rest = jnp.concatenate(
                (density[place, :, 128:], jnp.zeros((length, 64), jnp.float32)), axis=1
            )
            high = jnp.where(lanes_of(low) < 32, moved(low, 32), moved(rest, 32))
            return jnp.where(own, low, high) if which else jnp.where(own, high, low)

        return planes

    pack(one_half(True), 12, 96, pair, alone, kept)
    pack(one_half(False), 12, 96, pair, alone, given)


def frequencies(length, first, lanes, first_lane):
    rows = lax.broadcasted_iota(jnp.int32, (length, lanes), 0)
    columns = lax.broadcasted_iota(jnp.int32, (length, lanes), 1) + first_lane
    row = jnp.where(rows < length // 2, rows, rows - length).astype(jnp.float32)
    column = jnp.where(columns < length // 2, columns, columns - length).astype(jnp.float32)
    outer = jnp.where(first < length // 2, first, first - length).astype(jnp.float32)
    return 0.5 * RECIPROCAL_SQUARE * (outer * outer + row * row + column * column)


def inner_kernel(slab, me, energies, orbitals, responses, inner):
    length = orbitals.shape[4]
    step = pl.program_id(0)

    @pl.when(step == 0)
    def _():
        inner[...] = jnp.zeros_like(inner)

    for one in range(2):
        kinetic = frequencies(length, me[0] * slab + 2 * step + one, length, 0)
        for band in range(2):
            shifted = kinetic - energies[0, band]
            real = shifted * responses[0, band, 0, one]
            imag = shifted * responses[0, band, 1, one]
            for other in range(2):
                left_real, left_imag = orbitals[0, other, 0, one], orbitals[0, other, 1, one]
                inner[0, other, band] += folded(left_real * real + left_imag * imag)
                inner[1, other, band] += folded(left_real * imag - left_imag * real)


def direct_kernel(slab, me, energies, inner, orbitals, responses, out):
    length = orbitals.shape[4]
    cells = float(length**3)
    for one in range(2):
        kinetic = frequencies(length, me[0] * slab + 2 * pl.program_id(0) + one, length, 0)
        inverse = 1.0 / (1.0 + kinetic)
        for band in range(2):
            shifted = kinetic - energies[0, band]
            real = shifted * responses[0, band, 0, one]
            imag = shifted * responses[0, band, 1, one]
            for other in range(2):
                left_real, left_imag = orbitals[0, other, 0, one], orbitals[0, other, 1, one]
                by_real = inner[0, other, band] / cells
                by_imag = inner[1, other, band] / cells
                real = real - (left_real * by_real - left_imag * by_imag)
                imag = imag - (left_real * by_imag + left_imag * by_real)
            out[0, band, 0, one] = responses[0, band, 0, one] - real * inverse
            out[0, band, 1, one] = responses[0, band, 1, one] - imag * inverse


def finish_kernel(slab, starts, stride, tail, me, got, receive, base, out):
    length = base.shape[4]
    first = 2 * pl.program_id(0)
    parts_of = [(got, start, stride) for start in starts]
    planes = [plane(parts_of, first + one, slab, not tail, tail) for one in range(2)]
    values = [jnp.concatenate(both, axis=1) for both in zip(*planes)]
    applied = dot_receive(receive, values)
    for one in range(2):
        kinetic = frequencies(length, me[0] * slab + first + one, 128, 128 if tail else 0)
        inverse = 1.0 / (1.0 + kinetic)
        for part in range(2):
            piece = applied[part][:, 128 * one : 128 * (one + 1)]
            out[0, 0, part, one] = base[0, 0, part, one] - piece * inverse


def mirror_kernel(me, got, single, pair, alone, out, natural, loose):
    below = me[0] < out.shape[0] // 2
    for place in range(12):
        loose[place] = unpack(got, place, 12, 96, 112)
        natural[place] = dot_mirror(single[...], loose[place])

    def planes(place):
        values = loose[place % 12]
        other = moved(values, -48)
        return jnp.where(below, values, other) if place < 12 else jnp.where(below, other, values)

    pack(planes, 13, 48, pair, alone, out)


def swap_kernel(got, order, natural, out):
    length = natural.shape[1]
    for place in range(12):
        halves_of = dot_mirror(order[...], unpack(got, place, 13, 48, 64))
        low, high = halves_of[:length], moved(halves_of[length:], 48)
        swapped = jnp.where(lanes_of(low) < 48, low, high)
        out[place] = (natural[place] + swapped) * 0.125


def cost(flops, moved):
    return pl.CostEstimate(flops=int(flops), bytes_accessed=int(moved), transcendentals=0)


def whole():
    return pl.BlockSpec(memory_space=pltpu.VMEM)


def scalars():
    return pl.BlockSpec(memory_space=pltpu.SMEM)


def call(kernel, name, grid, ins, outs, shapes, estimate, aliases=None, scratch=()):
    return pl.pallas_call(
        kernel,
        grid=(grid,),
        in_specs=ins,
        out_specs=outs,
        out_shape=shapes,
        compiler_params=pltpu.CompilerParams(
            dimension_semantics=("arbitrary",), vmem_limit_bytes=VMEM_BYTES
        ),
        cost_estimate=estimate,
        input_output_aliases=aliases or {},
        scratch_shapes=scratch,
        name=name,
    )


def f32(*shape):
    return jax.ShapeDtypeStruct(shape, jnp.float32)


def packed_body(orbitals, responses, energies, weights, potential, perturbation):
    length = orbitals.shape[-1]
    slab = orbitals.shape[3]
    members = length // slab
    pairs = slab // 2
    rows = 2 * slab
    table = {key: jnp.asarray(value) for key, value in matrices(length, slab, members).items()}
    me = lax.axis_index("pw").astype(jnp.int32).reshape(1)
    pool = lax.axis_index("pool").astype(jnp.int32).reshape(1)
    field_bytes = 4 * members * pairs * 3 * rows * 128
    stage_flops = 6 * 2 * 2 * length * length * length * slab * 2

    half_spec = pl.BlockSpec((members, 1, 3, rows, 128), lambda p: (0, p, 0, 0, 0))
    half_shape = f32(members, pairs, 3, rows, 128)

    def exchange(values, after=None):
        values = values.reshape(members, -1, 128)
        if after is not None:
            values, _ = lax.optimization_barrier((values, after))
        return lax.all_to_all(values, "pw", split_axis=0, concat_axis=0, tiled=True)

    def to_half(field, band, slots, group=None, into=None, slot=0):
        def kernel(field, cosine, mixed, send, *rest):
            to_half_kernel(field, cosine, mixed, send, *rest[-2:])

        if group is None:
            grid = pairs
            pair_at = lambda p: p
            block_at = lambda p: (0, p // 2, slot + p % 2, 0, 0, 0)
        else:
            grid = pairs // 2
            pair_at = lambda p: 2 * p + group
            block_at = lambda p: (0, p, slot, 0, 0, 0)
        return call(
            kernel,
            "to_half",
            grid,
            [
                pl.BlockSpec(
                    (1, 1, 2, 2, length, length), lambda p: (0, band, 0, pair_at(p), 0, 0)
                ),
                whole(),
                whole(),
                whole(),
            ]
            + ([] if into is None else [pl.BlockSpec(memory_space=pl.ANY)]),
            pl.BlockSpec((members, 1, 1, 3, rows, 128), block_at),
            f32(members, pairs // 2, slots, 3, rows, 128),
            cost(2 * stage_flops * grid / pairs, 2 * field_bytes * grid / pairs),
            {} if into is None else {4: 0},
            [pltpu.VMEM((2, 2, 2 * length, 128), jnp.float32)],
        )(
            field, table["cosine"], table["mixed"], table["inverse_send"],
            *(() if into is None else (into,)),
        )

    def to_space(gots, starts, strides):
        return call(
            functools.partial(to_space_kernel, slab, starts, strides),
            "to_space",
            pairs,
            [whole()] * (len(gots) + 1),
            pl.BlockSpec((2, 2 * length, length), lambda p: (p, 0, 0)),
            f32(slab, 2 * length, length),
            cost(stage_flops, 2 * field_bytes),
        )(*(got.reshape(-1, 128) for got in gots), table["inverse_receive"])

    plane_spec = pl.BlockSpec((2, length, length), lambda p: (p, 0, 0))
    send_specs = [
        pl.BlockSpec((members, 1, 2, rows, 128), lambda p: (0, p, 0, 0, 0)),
        pl.BlockSpec((members, 1, rows, 128), lambda p: (0, p, 0, 0)),
    ]
    send_shapes = [
        f32(members, pairs, 2, rows, 128),
        f32(members, pairs, rows, 128),
    ]
    block_shape = f32(members, 112, 128)
    inner_spec = pl.BlockSpec((2, 2, 8, length), lambda p: (0, 0, 0, 0))

    def apply_first(got, spaces, field, change):
        def kernel(weights, got, first, second, field, change, *tables_and_outs):
            receive, cosine, mixed, send, main, inner, density = tables_and_outs
            apply_kernel(
                slab, (9 * rows, 12 * rows), 15 * rows, 0, weights, got, Both(first, second), field, change, None,
                receive, cosine, mixed, send, main, None, inner, density,
            )

        return call(
            kernel,
            "apply_first",
            pairs,
            [scalars(), whole(), space_spec, space_spec, plane_spec, plane_spec] + [whole()] * 4,
            [half_spec, inner_spec, plane_spec],
            [half_shape, f32(2, 2, 8, length), f32(slab, length, length)],
            cost(3 * stage_flops, 5 * field_bytes),
        )(
            weights, got.reshape(-1, 128), *spaces, field, change,
            table["inverse_receive"], table["cosine"], table["mixed"], table["forward_send"],
        )

    def apply_last(got, spaces, field, change, before):
        def kernel(weights, got, first, second, field, change, before, *tables_and_outs):
            receive, cosine, mixed, send, main, tail, inner, density = tables_and_outs
            apply_kernel(
                slab, (0, 3 * rows), 6 * rows, 1, weights, got, Both(first, second), field, change, before,
                receive, cosine, mixed, send, main, tail, inner, density,
            )

        return call(
            kernel,
            "apply_last",
            pairs,
            [scalars(), whole(), space_spec, space_spec] + [plane_spec] * 3 + [whole()] * 4,
            send_specs + [inner_spec, plane_spec],
            send_shapes + [f32(2, 2, 8, length), f32(slab, length, length)],
            cost(3 * stage_flops, 5 * field_bytes),
        )(
            weights, got.reshape(-1, 128), *spaces, field, change, before,
            table["inverse_receive"], table["cosine"], table["mixed"], table["forward_send"],
        )

    space_spec = pl.BlockSpec((2, 2 * length, length), lambda p: (p, 0, 0))
    bands_spec = pl.BlockSpec((1, 2, 2, 2, length, length), lambda p: (0, 0, 0, p, 0, 0))

    def finish(base, got, band, starts, stride, tail):
        lane_block = 1 if tail else 0
        one_spec = pl.BlockSpec(
            (1, 1, 2, 2, length, 128), lambda p: (0, band, 0, p, 0, lane_block)
        )
        return call(
            functools.partial(finish_kernel, slab, starts, stride, tail),
            "finish",
            pairs,
            [scalars(), whole(), whole(), one_spec],
            one_spec,
            f32(*base.shape),
            cost(stage_flops, 2 * field_bytes),
            {3: 0},
        )(me, got.reshape(-1, 128), table["forward_receive"], base)

    field = jnp.transpose(potential, (1, 0, 2))
    change = jnp.transpose(perturbation, (1, 0, 2))
    got_one = exchange(to_half(orbitals, 0, 1, 0))
    half_two = to_half(orbitals, 0, 5, 1)
    half_two = to_half(orbitals, 1, 5, None, half_two, 1)
    got_two = exchange(to_half(responses, 0, 5, None, half_two, 3), got_one)
    direct_inner = call(
        functools.partial(inner_kernel, slab),
        "inner",
        pairs,
        [scalars(), scalars(), bands_spec, bands_spec],
        pl.BlockSpec((2, 2, 2, 8, length), lambda p: (0, 0, 0, 0, 0)),
        f32(2, 2, 2, 8, length),
        cost(32 * field_bytes, 4 * field_bytes),
    )(me, energies, orbitals, responses)
    got_last = exchange(to_half(responses, 1, 2), (got_two, direct_inner))
    spaces = [
        to_space([got_one, got_two], (0, 0), (3 * rows, 15 * rows)),
        to_space([got_two], (3 * rows, 6 * rows), (15 * rows, 15 * rows)),
    ]
    send_first, inner_first, before = apply_first(got_two, spaces, field, change)
    back_first = exchange(send_first, got_last)
    last_main, last_tail, inner_last, density = apply_last(
        got_last, spaces, field, change, before
    )
    kept, given = call(
        pack_kernel,
        "pack",
        1,
        [scalars(), whole(), whole(), whole()],
        [whole(), whole()],
        [block_shape, block_shape],
        cost(4e9, 5e6),
    )(pool, density, table["pair"], table["alone"])
    swap = [(0, 1), (1, 0)]
    local_inner = direct_inner + jnp.stack((inner_first, inner_last), axis=2)
    riding = jnp.sum(local_inner, axis=(3, 4)).reshape(1, 1, 8)
    riding = jnp.pad(riding, ((0, 0), (0, 0), (0, 120)))
    row = lax.broadcasted_iota(jnp.int32, block_shape.shape, 1)
    summed = jnp.where(row < 108, kept + lax.ppermute(given, "pool", swap), riding)
    got_density = exchange(summed, back_first)
    inner = jnp.sum(got_density[:, 108, :8], axis=0).reshape(2, 2, 2)
    back_tail = exchange(last_tail, got_density)
    base = call(
        functools.partial(direct_kernel, slab),
        "direct",
        pairs,
        [scalars(), scalars(), scalars(), bands_spec, bands_spec],
        bands_spec,
        f32(*responses.shape),
        cost(32 * field_bytes, 6 * field_bytes),
    )(me, energies, inner, orbitals, responses)
    mirrored, natural = call(
        mirror_kernel,
        "mirror",
        1,
        [scalars()] + [whole()] * 4,
        [whole(), whole()],
        [f32(members, 64, 128), f32(slab, length, 128)],
        cost(4e9, 4e6),
        scratch=[pltpu.VMEM((slab, length, 128), jnp.float32)],
    )(
        me, got_density.reshape(-1, 128),
        table["loose_mirror"], table["loose_pair"], table["loose_alone"],
    )
    got_mirrored = exchange(mirrored, (back_tail, base))
    base = finish(base, back_first, 0, (0, 3 * rows), 6 * rows, False)
    back_main = exchange(last_main, (got_mirrored, base))
    symmetric = call(
        swap_kernel,
        "swap",
        1,
        [whole()] * 3,
        whole(),
        f32(slab, length, 128),
        cost(1e9, 4e6),
    )(got_mirrored.reshape(-1, 128), table["swapped"], natural)
    other = lax.ppermute(symmetric, "pool", swap)
    low = jnp.where(pool == 0, symmetric, other)
    high = jnp.where(pool == 0, other, symmetric)
    response_density = jnp.concatenate((low[..., :96], high[..., :96]), axis=2)
    base = finish(base, back_first, 0, (2 * rows, 5 * rows), 6 * rows, True)
    base = finish(base, back_tail, 1, (0, rows), 2 * rows, True)
    base, response_density, back_main = lax.optimization_barrier(
        (base, response_density, back_main)
    )
    base = finish(base, back_main, 1, (0, 2 * rows), 4 * rows, False)
    return base, response_density


class Both:
    def __init__(self, *refs):
        self.refs = refs

    def __getitem__(self, index):
        return self.refs[index[0]][index[1:]]


def tables(length):
    indices = jnp.arange(length, dtype=jnp.int32)
    angles = (indices[:, None] * indices[None, :] % length).astype(jnp.float32) * (
        2.0 * math.pi / length
    )
    factor = 1.0 / math.sqrt(length)
    return (jnp.cos(angles) * factor, jnp.sin(angles) * factor)


def apply_table(values, table_in, along_axis):
    rotated = jnp.tensordot(
        values, table_in, axes=((along_axis,), (0,)), precision=lax.Precision.HIGHEST
    )
    return jnp.moveaxis(rotated, -1, along_axis)


def transform(field_in, along_axis, cosine_table, sine_table, phase_sign):
    real_part = field_in[:, :, 0]
    imag_part = field_in[:, :, 1]
    real_cos = apply_table(real_part, cosine_table, along_axis)
    real_sin = apply_table(real_part, sine_table, along_axis)
    imag_cos = apply_table(imag_part, cosine_table, along_axis)
    imag_sin = apply_table(imag_part, sine_table, along_axis)
    return jnp.stack((real_cos - phase_sign * imag_sin, phase_sign * real_sin + imag_cos), axis=2)


def signed_freq(indices, length):
    return jnp.where(indices < length // 2, indices, indices - length).astype(jnp.float32)


def negated(values, along_axis):
    return jnp.roll(jnp.flip(values, along_axis), 1, along_axis)


def products(left_side, right_side):
    band_count = left_side.shape[0]
    highest = lax.Precision.HIGHEST
    left_real = left_side[:, 0].reshape(band_count, -1)
    left_imag = left_side[:, 1].reshape(band_count, -1)
    right_real = right_side[:, 0].reshape(band_count, -1)
    right_imag = right_side[:, 1].reshape(band_count, -1)
    real_sum = jnp.dot(left_real, right_real.T, precision=highest) + jnp.dot(
        left_imag, right_imag.T, precision=highest
    )
    imag_sum = jnp.dot(left_real, right_imag.T, precision=highest) - jnp.dot(
        left_imag, right_real.T, precision=highest
    )
    return (real_sum, imag_sum)


def plain_body(orbitals, responses, energies, weights, potential, perturbation):
    length = orbitals.shape[-1]
    slab_rows = orbitals.shape[3]
    cosine_table, sine_table = tables(length)

    def to_space(field_in):
        return transform(
            transform(field_in, 4, cosine_table, sine_table, 1.0), 3, cosine_table, sine_table, 1.0
        )

    def finish_one(one_piece):
        return transform(one_piece, 2, cosine_table, sine_table, 1.0)

    orbital_space = finish_one(
        lax.all_to_all(to_space(orbitals), "pw", split_axis=4, concat_axis=3, tiled=True)
    )
    response_space = finish_one(
        lax.all_to_all(to_space(responses), "pw", split_axis=4, concat_axis=3, tiled=True)
    )
    partial_value = (
        2.0
        * weights[0]
        * jnp.sum(
            orbital_space[0, :, 0] * response_space[0, :, 0]
            + orbital_space[0, :, 1] * response_space[0, :, 1],
            axis=0,
        )
    )
    applied_space = potential * response_space + perturbation * orbital_space
    first_row = lax.axis_index("pw") * slab_rows
    row_freq = signed_freq(first_row + jnp.arange(slab_rows, dtype=jnp.int32), length)
    full_freq = signed_freq(jnp.arange(length, dtype=jnp.int32), length)
    kinetic = (
        0.5
        * RECIPROCAL_SQUARE
        * (
            row_freq[:, None, None] * row_freq[:, None, None]
            + full_freq[None, :, None] * full_freq[None, :, None]
            + full_freq[None, None, :] * full_freq[None, None, :]
        )
    )
    shifted = kinetic[None] - energies[0][:, None, None, None]
    direct = shifted[None, :, None] * responses
    sectioned = transform(
        transform(applied_space, 4, cosine_table, sine_table, -1.0),
        2,
        cosine_table,
        sine_table,
        -1.0,
    )
    residual = direct + transform(
        lax.all_to_all(sectioned, "pw", split_axis=3, concat_axis=4, tiled=True),
        3,
        cosine_table,
        sine_table,
        -1.0,
    )
    over_real, over_imag = lax.psum(products(orbitals[0], residual[0]), "pw")
    highest = lax.Precision.HIGHEST
    orbital_real = orbitals[0, :, 0]
    orbital_imag = orbitals[0, :, 1]
    combine_real = jnp.einsum(
        "mn,mxyz->nxyz", over_real, orbital_real, precision=highest
    ) - jnp.einsum("mn,mxyz->nxyz", over_imag, orbital_imag, precision=highest)
    combine_imag = jnp.einsum(
        "mn,mxyz->nxyz", over_imag, orbital_real, precision=highest
    ) + jnp.einsum("mn,mxyz->nxyz", over_real, orbital_imag, precision=highest)
    cell_count = float(length**3)
    projected = residual - jnp.stack((combine_real, combine_imag), axis=1)[None] / cell_count
    new_responses = responses - projected / (1.0 + kinetic)[None, None, None]
    summed = lax.psum(partial_value, "pool")
    mirrored = summed + negated(summed, 0)
    row_slab = lax.all_to_all(mirrored, "pw", split_axis=0, concat_axis=1, tiled=True)
    signsum = row_slab + negated(row_slab, 1)
    swapped = lax.all_to_all(signsum, "pw", split_axis=1, concat_axis=0, tiled=True)
    total_sym = signsum + jnp.transpose(swapped, (1, 0, 2))
    return (new_responses, total_sym / 8.0)


def body(orbitals, responses, energies, weights, potential, perturbation):
    slab, length = orbitals.shape[3], orbitals.shape[-1]
    fits = slab == 12 and length == 192 and orbitals.shape[0] == 1 and orbitals.shape[1] == 2
    return (packed_body if fits else plain_body)(
        orbitals, responses, energies, weights, potential, perturbation
    )


def solution(mesh):
    placed = (
        P("pool", None, None, "pw", None, None),
        P("pool", None, None, "pw", None, None),
        P("pool", None),
        P("pool"),
        P(None, "pw", None),
        P(None, "pw", None),
    )
    return jax.shard_map(
        body,
        mesh=mesh,
        in_specs=placed,
        out_specs=(P("pool", None, None, "pw", None, None), P("pw", None, None)),
        check_vma=False,
    )
```

```python
import functools
import math

import jax
import jax.numpy as jnp
import ml_dtypes
import numpy as np
from jax import lax
from jax.experimental import pallas as pl
from jax.experimental.pallas import tpu as pltpu
from jax.sharding import PartitionSpec as P

RECIPROCAL_SQUARE = 0.023428
VMEM_BYTES = 63 * 1024 * 1024


def split_table(table):
    high = table.astype(ml_dtypes.bfloat16)
    low = (table - high.astype(np.float64)).astype(ml_dtypes.bfloat16)
    return np.stack((high, low))


def long_table(table):
    high, low = split_table(table)
    return np.concatenate((high, high, low), axis=1)


@functools.cache
def matrices(length, slab, members):
    index = np.arange(length)
    angles = (index[:, None] * index[None, :] % length) * (2.0 * math.pi / length)
    cosine = np.cos(angles) / math.sqrt(length)
    sine = np.sin(angles) / math.sqrt(length)
    lanes = 128 * -(-length // 128)
    pad = ((0, 0), (0, lanes - length))
    inverse = np.block([[cosine, -sine], [sine, cosine]])
    forward = np.block([[cosine, sine], [-sine, cosine]])
    sent = np.arange(2 * length).reshape(2, members, slab).transpose(1, 0, 2).reshape(-1)
    got = np.arange(2 * length).reshape(2, members, slab // 4, 2, 2).transpose(4, 0, 3, 1, 2)
    got = got.reshape(2, -1)
    first = np.arange(2 * length).reshape(2, 2, length // 2)[:, 0].reshape(-1)
    parity = np.arange(2 * length).reshape(length, 2).T
    mirror = np.eye(length) + np.eye(length)[(-index) % length]
    both = np.zeros((members, 2, slab, 2, length))
    for which in range(2):
        both[:, which, :, which, :] = mirror.reshape(members, slab, length)
    both = both.reshape(2 * length, 2, length)
    alone = np.pad(mirror.reshape(members, slab, length), ((0, 0), (0, 4), (0, 0)))
    alone = alone.reshape(-1, length)
    loose = index.reshape(members, slab).T.reshape(-1)
    fold = np.minimum(index, length - index)
    swapped = np.zeros((2, length, slab + 1, members))
    swapped[0, index, fold % slab, fold // slab] = 1.0
    swapped[0, length // 2] = 0.0
    swapped[0, length // 2, slab, members // 2] = 1.0
    folded = (length - fold) % length
    swapped[1, index, folded % slab, folded // slab] = 1.0
    swapped[1, 0] = 0.0
    swapped[1, 0, slab, 0] = 1.0
    return {
        "cosine": split_table(np.pad(cosine, pad)),
        "mixed": np.stack(
            [split_table(np.pad(sine + sign * cosine, pad)) for sign in (-1.0, 1.0)]
        ),
        "inverse_send": np.stack([long_table(inverse[sent[:length]][:, one]) for one in parity]),
        "inverse_receive": np.stack([long_table(inverse[first][:, one]) for one in got]),
        "forward_send": long_table(forward[sent]),
        "forward_receive": np.stack([long_table(forward[first][:, one]) for one in got]),
        "pair": both.reshape(2 * length, -1).astype(ml_dtypes.bfloat16),
        "alone": alone.astype(ml_dtypes.bfloat16),
        "loose_pair": both[:, :, loose].reshape(2 * length, -1).astype(ml_dtypes.bfloat16),
        "loose_alone": alone[:, loose].astype(ml_dtypes.bfloat16),
        "loose_mirror": mirror[:, loose].astype(ml_dtypes.bfloat16),
        "swapped": swapped.reshape(2 * length, -1).astype(ml_dtypes.bfloat16),
    }


def halves(values):
    high = values.astype(jnp.bfloat16)
    return high, (values - high.astype(jnp.float32)).astype(jnp.bfloat16)


def dot(left, right):
    return lax.dot_general(
        left, right, (((1,), (0,)), ((), ())), preferred_element_type=jnp.float32
    )


def dot_right(values, table):
    high, low = halves(values)
    return dot(high, table[0]) + (dot(high, table[1]) + dot(low, table[0]))


def dot_left(table, values):
    high, low = halves(values)
    return dot(table, jnp.concatenate((high, low, high), axis=0))


def turn_lanes(real, imag, cosine, mixed, sign):
    common = dot_right(real + imag, cosine)
    if sign > 0:
        return common - dot_right(imag, mixed.at[1]), common + dot_right(real, mixed.at[0])
    return common + dot_right(imag, mixed.at[0]), common - dot_right(real, mixed.at[1])


def half_lengths(even, odd):
    return even + odd, even - odd


def dot_receive(table, found):
    first, second = half_lengths(*(dot_left(table[one], found[one]) for one in range(2)))
    mid = first.shape[0] // 2
    return (
        jnp.concatenate((first[:mid], second[:mid]), axis=0),
        jnp.concatenate((first[mid:], second[mid:]), axis=0),
    )


def dot_mirror(table, values):
    high, low = halves(values)
    return dot(table, high) + dot(table, low)


def merge_tails(first, second):
    return first + pltpu.roll(second, 64, 1)


def to_half_kernel(field, cosine, mixed, send, out, turned):
    pair, length = field.shape[3], field.shape[4]
    members, rows = out.shape[0], out.shape[-2]
    mid = members // 2
    out = out.at[:, 0, 0]
    parts = [field[0, 0, part].reshape(pair * length, length) for part in range(2)]
    parts = turn_lanes(*parts, cosine, mixed, 1)
    for part in range(2):
        turned[part, 0] = parts[part][:, :128]
        turned[part, 1] = parts[part][:, 128:]
    tails = []
    for one in range(pair):
        found = []
        for parity in range(2):
            rows_of = pl.ds(one * length + parity, length // 2, stride=2)
            found.append(
                jnp.concatenate(
                    [
                        jnp.concatenate((turned[part, 0, rows_of], turned[part, 1, rows_of]), axis=1)
                        for part in range(2)
                    ],
                    axis=0,
                )
            )
        done = half_lengths(*(dot_left(send[parity], found[parity]) for parity in range(2)))
        for half in range(2):
            to = slice(half * mid, (half + 1) * mid)
            out[to, one] = done[half][:, :128].reshape(mid, rows, 128)
        tails.append([piece[:, 128:] for piece in done])
    for half in range(2):
        to = slice(half * mid, (half + 1) * mid)
        out[to, 2] = merge_tails(tails[0][half], tails[1][half]).reshape(mid, rows, 128)


def received(ref, start, stride, count):
    return ref[pl.ds(start, count, stride=stride), :]


def plane(parts_of, place, slab, with_main, with_tail):
    def rows_at(row):
        pieces = [
            received(ref, start + row, stride, ref.shape[0] // stride)
            for ref, start, stride in parts_of
        ]
        return jnp.concatenate(pieces, axis=0)

    found = [[], []]
    for part in range(2):
        row = part * slab + place
        mains, tails = [None, None], [None, None]
        if with_main:
            mains = [rows_at(one * 2 * slab + row) for one in range(2)]
            row = row + 4 * slab
        if with_tail:
            tail = rows_at(row)
            tails = [tail, pltpu.roll(tail, 64, 1)]
        for one in range(2):
            pieces = [piece for piece in (mains[one], tails[one]) if piece is not None]
            found[one].append(jnp.concatenate(pieces, axis=1) if len(pieces) > 1 else pieces[0])
    return [jnp.concatenate(one, axis=0) for one in found]


def to_space_kernel(slab, starts, strides, *refs):
    *gots, receive, space = refs
    length = space.shape[2]
    parts_of = list(zip(gots if len(gots) > 1 else gots * 2, starts, strides))
    for one in range(2):
        place = 2 * pl.program_id(0) + one
        values = plane(parts_of, place, slab, True, True)
        real, imag = dot_receive(receive, values)
        space[one, :length] = real[:, :length]
        space[one, length:] = imag[:, :length]


def folded(values):
    return values.reshape(-1, 8, values.shape[-1]).sum(axis=0)


def apply_kernel(
    slab, starts, stride, band, weights, got, spaces, potential, perturbation, before,
    receive, cosine, mixed, send, out_main, out_tail, inner, density
):
    length = potential.shape[1]
    members, rows = out_main.shape[0], out_main.shape[3]
    step = pl.program_id(0)
    twice_weight = 2.0 * weights[0]

    @pl.when(step == 0)
    def _():
        inner[...] = jnp.zeros_like(inner)

    tails = []
    sums = []
    for one in range(2):
        parts_of = [(got, start, stride) for start in starts]
        values = plane(parts_of, 2 * step + one, slab, True, True)
        real, imag = (piece[:, :length] for piece in dot_receive(receive, values))
        own_real, own_imag = spaces[band, one, :length], spaces[band, one, length:]
        local = twice_weight * (own_real * real + own_imag * imag)
        if before is not None:
            local = local + before[one]
        sums.append(local)
        field, change = potential[one], perturbation[one]
        real = field * real + change * own_real
        imag = field * imag + change * own_imag
        for other in range(2):
            left_real, left_imag = spaces[other, one, :length], spaces[other, one, length:]
            inner[0, other] += folded(left_real * real + left_imag * imag)
            inner[1, other] += folded(left_real * imag - left_imag * real)
        turned = jnp.concatenate(turn_lanes(real, imag, cosine, mixed, -1), axis=0)
        done = dot_left(send[...], turned)
        out_main[:, 0, one] = done[:, :128].reshape(members, rows, 128)
        tails.append(done[:, 128:])
    tail = merge_tails(*tails).reshape(members, rows, 128)
    if out_tail is None:
        out_main[:, 0, 2] = tail
    else:
        out_tail[:, 0] = tail
    for one in range(2):
        density[one] = sums[one]


def lanes_of(values):
    return lax.broadcasted_iota(jnp.int32, values.shape, 1)


def moved(values, by):
    return pltpu.roll(values, by % 128, 1) if by % 128 else values


def pack(planes, count, width, pair, alone, out):
    members = out.shape[0]
    blocks = []
    for block in range(-(-count * width // 128)):
        made = None
        for place in range(count):
            start = place * width - 128 * block
            if start >= 128 or start + width <= 0:
                continue
            values = moved(planes(place), start)
            made = values if made is None else jnp.where(lanes_of(values) < start, made, values)
        blocks.append(made)
    for first in range(0, len(blocks) - 1, 2):
        out[:, 12 * first : 12 * first + 24] = dot_mirror(
            pair[...], jnp.concatenate(blocks[first : first + 2], axis=0)
        ).reshape(members, 24, 128)
    out[:, 12 * len(blocks) - 12 :] = dot_mirror(alone[...], blocks[-1]).reshape(members, 16, 128)


def unpack(got, place, count, width, rows, row_at=lambda row: row):
    members = got.shape[0] // rows
    blocks = [
        received(got, row_at(12 * block + place), rows, members)
        for block in range(-(-count * width // 128))
    ]
    found = []
    for one in range(count):
        block, start = divmod(one * width, 128)
        values = moved(blocks[block], -start)
        if start + width > 128:
            rest = moved(blocks[block + 1], -start)
            values = jnp.where(lanes_of(values) < 128 - start, values, rest)
        found.append(values)
    return jnp.concatenate(found, axis=0)


def pack_kernel(pool, density, pair, alone, kept, given):
    length = density.shape[1]
    own = pool[0] == 0

    def one_half(which):
        def planes(place):
            low = density[place, :, :128]
            rest = jnp.concatenate(
                (density[place, :, 128:], jnp.zeros((length, 64), jnp.float32)), axis=1
            )
            high = jnp.where(lanes_of(low) < 32, moved(low, 32), moved(rest, 32))
            return jnp.where(own, low, high) if which else jnp.where(own, high, low)

        return planes

    pack(one_half(True), 12, 96, pair, alone, kept)
    pack(one_half(False), 12, 96, pair, alone, given)


def frequencies(length, first, lanes, first_lane):
    rows = lax.broadcasted_iota(jnp.int32, (length, lanes), 0)
    columns = lax.broadcasted_iota(jnp.int32, (length, lanes), 1) + first_lane
    row = jnp.where(rows < length // 2, rows, rows - length).astype(jnp.float32)
    column = jnp.where(columns < length // 2, columns, columns - length).astype(jnp.float32)
    outer = jnp.where(first < length // 2, first, first - length).astype(jnp.float32)
    return 0.5 * RECIPROCAL_SQUARE * (outer * outer + row * row + column * column)


def inner_kernel(slab, me, energies, orbitals, responses, inner):
    length = orbitals.shape[4]
    step = pl.program_id(0)

    @pl.when(step == 0)
    def _():
        inner[...] = jnp.zeros_like(inner)

    for one in range(2):
        kinetic = frequencies(length, me[0] * slab + 2 * step + one, length, 0)
        for band in range(2):
            shifted = kinetic - energies[0, band]
            real = shifted * responses[0, band, 0, one]
            imag = shifted * responses[0, band, 1, one]
            for other in range(2):
                left_real, left_imag = orbitals[0, other, 0, one], orbitals[0, other, 1, one]
                inner[0, other, band] += folded(left_real * real + left_imag * imag)
                inner[1, other, band] += folded(left_real * imag - left_imag * real)


def direct_kernel(slab, me, energies, inner, orbitals, responses, out):
    length = orbitals.shape[4]
    cells = float(length**3)
    for one in range(2):
        kinetic = frequencies(length, me[0] * slab + 2 * pl.program_id(0) + one, length, 0)
        inverse = 1.0 / (1.0 + kinetic)
        for band in range(2):
            shifted = kinetic - energies[0, band]
            real = shifted * responses[0, band, 0, one]
            imag = shifted * responses[0, band, 1, one]
            for other in range(2):
                left_real, left_imag = orbitals[0, other, 0, one], orbitals[0, other, 1, one]
                by_real = inner[0, other, band] / cells
                by_imag = inner[1, other, band] / cells
                real = real - (left_real * by_real - left_imag * by_imag)
                imag = imag - (left_real * by_imag + left_imag * by_real)
            out[0, band, 0, one] = responses[0, band, 0, one] - real * inverse
            out[0, band, 1, one] = responses[0, band, 1, one] - imag * inverse


def finish_kernel(slab, starts, stride, tail, me, got, receive, base, out):
    length, count = base.shape[4], base.shape[3]
    parts_of = [(got, start, stride) for start in starts]
    for pair in range(0, count, 2):
        first = count * pl.program_id(0) + pair
        planes = [plane(parts_of, first + one, slab, not tail, tail) for one in range(2)]
        values = [jnp.concatenate(both, axis=1) for both in zip(*planes)]
        applied = dot_receive(receive, values)
        for one in range(2):
            kinetic = frequencies(length, me[0] * slab + first + one, 128, 128 if tail else 0)
            inverse = 1.0 / (1.0 + kinetic)
            for part in range(2):
                piece = applied[part][:, 128 * one : 128 * (one + 1)]
                out[0, 0, part, pair + one] = base[0, 0, part, pair + one] - piece * inverse


def mixed_row(row):
    return row // 40 * 88 + 48 + row % 40


def mirror_kernel(me, got, pair, alone, out, loose):
    below = me[0] < out.shape[0] // 2
    for place in range(12):
        loose[place] = unpack(got, place, 12, 96, 264, mixed_row)

    def planes(place):
        values = loose[place % 12]
        other = moved(values, -48)
        return jnp.where(below, values, other) if place < 12 else jnp.where(below, other, values)

    pack(planes, 13, 48, pair, alone, out)


def swap_kernel(got, got_swapped, single, order, out):
    length = out.shape[1]
    for place in range(12):
        own = dot_mirror(single[...], unpack(got, place, 12, 96, 264, mixed_row))
        halves_of = dot_mirror(order[...], unpack(got_swapped, place, 13, 48, 64))
        low, high = halves_of[:length], moved(halves_of[length:], 48)
        swapped = jnp.where(lanes_of(low) < 48, low, high)
        out[place] = (own + swapped) * 0.125


def cost(flops, moved):
    return pl.CostEstimate(flops=int(flops), bytes_accessed=int(moved), transcendentals=0)


def whole():
    return pl.BlockSpec(memory_space=pltpu.VMEM)


def scalars():
    return pl.BlockSpec(memory_space=pltpu.SMEM)


def call(kernel, name, grid, ins, outs, shapes, estimate, aliases=None, scratch=()):
    return pl.pallas_call(
        kernel,
        grid=(grid,),
        in_specs=ins,
        out_specs=outs,
        out_shape=shapes,
        compiler_params=pltpu.CompilerParams(
            dimension_semantics=("arbitrary",), vmem_limit_bytes=VMEM_BYTES
        ),
        cost_estimate=estimate,
        input_output_aliases=aliases or {},
        scratch_shapes=scratch,
        name=name,
    )


def f32(*shape):
    return jax.ShapeDtypeStruct(shape, jnp.float32)


def packed_body(orbitals, responses, energies, weights, potential, perturbation):
    length = orbitals.shape[-1]
    slab = orbitals.shape[3]
    members = length // slab
    pairs = slab // 2
    rows = 2 * slab
    table = {key: jnp.asarray(value) for key, value in matrices(length, slab, members).items()}
    me = lax.axis_index("pw").astype(jnp.int32).reshape(1)
    pool = lax.axis_index("pool").astype(jnp.int32).reshape(1)
    field_bytes = 4 * members * pairs * 3 * rows * 128
    stage_flops = 6 * 2 * 2 * length * length * length * slab * 2

    half_spec = pl.BlockSpec((members, 1, 3, rows, 128), lambda p: (0, p, 0, 0, 0))
    half_shape = f32(members, pairs, 3, rows, 128)

    def exchange(values, after=None):
        values = values.reshape(members, -1, 128)
        if after is not None:
            values, _ = lax.optimization_barrier((values, after))
        return lax.all_to_all(values, "pw", split_axis=0, concat_axis=0, tiled=True)

    def to_half(field, band, slots, group=None, into=None, slot=0):
        def kernel(field, cosine, mixed, send, *rest):
            to_half_kernel(field, cosine, mixed, send, *rest[-2:])

        if group is None:
            grid = pairs
            pair_at = lambda p: p
            block_at = lambda p: (0, p // 2, slot + p % 2, 0, 0, 0)
        else:
            grid = pairs // 2
            pair_at = lambda p: 2 * p + group
            block_at = lambda p: (0, p, slot, 0, 0, 0)
        return call(
            kernel,
            "to_half",
            grid,
            [
                pl.BlockSpec(
                    (1, 1, 2, 2, length, length), lambda p: (0, band, 0, pair_at(p), 0, 0)
                ),
                whole(),
                whole(),
                whole(),
            ]
            + ([] if into is None else [pl.BlockSpec(memory_space=pl.ANY)]),
            pl.BlockSpec((members, 1, 1, 3, rows, 128), block_at),
            f32(members, pairs // 2, slots, 3, rows, 128),
            cost(2 * stage_flops * grid / pairs, 2 * field_bytes * grid / pairs),
            {} if into is None else {4: 0},
            [pltpu.VMEM((2, 2, 2 * length, 128), jnp.float32)],
        )(
            field, table["cosine"], table["mixed"], table["inverse_send"],
            *(() if into is None else (into,)),
        )

    def to_space(gots, starts, strides):
        return call(
            functools.partial(to_space_kernel, slab, starts, strides),
            "to_space",
            pairs,
            [whole()] * (len(gots) + 1),
            pl.BlockSpec((2, 2 * length, length), lambda p: (p, 0, 0)),
            f32(slab, 2 * length, length),
            cost(stage_flops, 2 * field_bytes),
        )(*(got.reshape(-1, 128) for got in gots), table["inverse_receive"])

    plane_spec = pl.BlockSpec((2, length, length), lambda p: (p, 0, 0))
    send_specs = [
        pl.BlockSpec((members, 1, 2, rows, 128), lambda p: (0, p, 0, 0, 0)),
        pl.BlockSpec((members, 1, rows, 128), lambda p: (0, p, 0, 0)),
    ]
    send_shapes = [
        f32(members, pairs, 2, rows, 128),
        f32(members, pairs, rows, 128),
    ]
    block_shape = f32(members, 112, 128)
    inner_spec = pl.BlockSpec((2, 2, 8, length), lambda p: (0, 0, 0, 0))

    def apply_first(got, spaces, field, change):
        def kernel(weights, got, first, second, field, change, *tables_and_outs):
            receive, cosine, mixed, send, main, inner, density = tables_and_outs
            apply_kernel(
                slab, (9 * rows, 12 * rows), 15 * rows, 0, weights, got, Both(first, second), field, change, None,
                receive, cosine, mixed, send, main, None, inner, density,
            )

        return call(
            kernel,
            "apply_first",
            pairs,
            [scalars(), whole(), space_spec, space_spec, plane_spec, plane_spec] + [whole()] * 4,
            [half_spec, inner_spec, plane_spec],
            [half_shape, f32(2, 2, 8, length), f32(slab, length, length)],
            cost(3 * stage_flops, 5 * field_bytes),
        )(
            weights, got.reshape(-1, 128), *spaces, field, change,
            table["inverse_receive"], table["cosine"], table["mixed"], table["forward_send"],
        )

    def apply_last(got, spaces, field, change, before):
        def kernel(weights, got, first, second, field, change, before, *tables_and_outs):
            receive, cosine, mixed, send, main, tail, inner, density = tables_and_outs
            apply_kernel(
                slab, (0, 3 * rows), 6 * rows, 1, weights, got, Both(first, second), field, change, before,
                receive, cosine, mixed, send, main, tail, inner, density,
            )

        return call(
            kernel,
            "apply_last",
            pairs,
            [scalars(), whole(), space_spec, space_spec] + [plane_spec] * 3 + [whole()] * 4,
            send_specs + [inner_spec, plane_spec],
            send_shapes + [f32(2, 2, 8, length), f32(slab, length, length)],
            cost(3 * stage_flops, 5 * field_bytes),
        )(
            weights, got.reshape(-1, 128), *spaces, field, change, before,
            table["inverse_receive"], table["cosine"], table["mixed"], table["forward_send"],
        )

    space_spec = pl.BlockSpec((2, 2 * length, length), lambda p: (p, 0, 0))
    bands_spec = pl.BlockSpec((1, 2, 2, 2, length, length), lambda p: (0, 0, 0, p, 0, 0))

    def finish(base, got, band, starts, stride, tail):
        lane_block = 1 if tail else 0
        one_spec = pl.BlockSpec(
            (1, 1, 2, slab // 2, length, 128), lambda p: (0, band, 0, p, 0, lane_block)
        )
        return call(
            functools.partial(finish_kernel, slab, starts, stride, tail),
            "finish",
            2,
            [scalars(), whole(), whole(), one_spec],
            one_spec,
            f32(*base.shape),
            cost(stage_flops, 2 * field_bytes),
            {3: 0},
        )(me, got.reshape(-1, 128), table["forward_receive"], base)

    field = jnp.transpose(potential, (1, 0, 2))
    change = jnp.transpose(perturbation, (1, 0, 2))
    got_one = exchange(to_half(orbitals, 0, 1, 0))
    half_two = to_half(orbitals, 0, 5, 1)
    half_two = to_half(orbitals, 1, 5, None, half_two, 1)
    got_two = exchange(to_half(responses, 0, 5, None, half_two, 3), got_one)
    direct_inner = call(
        functools.partial(inner_kernel, slab),
        "inner",
        pairs,
        [scalars(), scalars(), bands_spec, bands_spec],
        pl.BlockSpec((2, 2, 2, 8, length), lambda p: (0, 0, 0, 0, 0)),
        f32(2, 2, 2, 8, length),
        cost(32 * field_bytes, 4 * field_bytes),
    )(me, energies, orbitals, responses)
    got_last = exchange(to_half(responses, 1, 2), (got_two, direct_inner))
    spaces = [
        to_space([got_one, got_two], (0, 0), (3 * rows, 15 * rows)),
        to_space([got_two], (3 * rows, 6 * rows), (15 * rows, 15 * rows)),
    ]
    send_first, inner_first, before = apply_first(got_two, spaces, field, change)
    back_first = exchange(send_first, got_last)
    last_main, last_tail, inner_last, density = apply_last(
        got_last, spaces, field, change, before
    )
    kept, given = call(
        pack_kernel,
        "pack",
        1,
        [scalars(), whole(), whole(), whole()],
        [whole(), whole()],
        [block_shape, block_shape],
        cost(4e9, 5e6),
    )(pool, density, table["pair"], table["alone"])
    swap = [(0, 1), (1, 0)]
    local_inner = direct_inner + jnp.stack((inner_first, inner_last), axis=2)
    riding = jnp.sum(local_inner, axis=(3, 4)).reshape(1, 1, 8)
    riding = jnp.pad(riding, ((0, 0), (0, 0), (0, 120)))
    row = lax.broadcasted_iota(jnp.int32, block_shape.shape, 1)
    summed = jnp.where(row < 108, kept + lax.ppermute(given, "pool", swap), riding)
    summed = jnp.pad(summed, ((0, 0), (0, 8), (0, 0))).reshape(members, 3, 40, 128)
    mixed = jnp.concatenate((last_tail.reshape(members, 3, 48, 128), summed), axis=2)
    got_mixed = exchange(mixed, back_first)
    inner = jnp.sum(got_mixed[:, mixed_row(108), :8], axis=0).reshape(2, 2, 2)
    base = call(
        functools.partial(direct_kernel, slab),
        "direct",
        pairs,
        [scalars(), scalars(), scalars(), bands_spec, bands_spec],
        bands_spec,
        f32(*responses.shape),
        cost(32 * field_bytes, 6 * field_bytes),
    )(me, energies, inner, orbitals, responses)
    mirrored = call(
        mirror_kernel,
        "mirror",
        1,
        [scalars()] + [whole()] * 3,
        whole(),
        f32(members, 64, 128),
        cost(2e9, 3e6),
        scratch=[pltpu.VMEM((slab, length, 128), jnp.float32)],
    )(me, got_mixed.reshape(-1, 128), table["loose_pair"], table["loose_alone"])
    got_mirrored = exchange(mirrored)
    base = finish(base, back_first, 0, (0, 3 * rows), 6 * rows, False)
    back_main = exchange(last_main, got_mirrored)
    symmetric = call(
        swap_kernel,
        "swap",
        1,
        [whole()] * 4,
        whole(),
        f32(slab, length, 128),
        cost(2e9, 5e6),
    )(
        got_mixed.reshape(-1, 128), got_mirrored.reshape(-1, 128),
        table["loose_mirror"], table["swapped"],
    )
    other = lax.ppermute(symmetric, "pool", swap)
    low = jnp.where(pool == 0, symmetric, other)
    high = jnp.where(pool == 0, other, symmetric)
    response_density = jnp.concatenate((low[..., :96], high[..., :96]), axis=2)
    base = finish(base, back_first, 0, (2 * rows, 5 * rows), 6 * rows, True)
    base = finish(base, got_mixed, 1, (0, rows), 88, True)
    base, response_density, back_main = lax.optimization_barrier(
        (base, response_density, back_main)
    )
    base = finish(base, back_main, 1, (0, 2 * rows), 4 * rows, False)
    return base, response_density


class Both:
    def __init__(self, *refs):
        self.refs = refs

    def __getitem__(self, index):
        return self.refs[index[0]][index[1:]]


def tables(length):
    indices = jnp.arange(length, dtype=jnp.int32)
    angles = (indices[:, None] * indices[None, :] % length).astype(jnp.float32) * (
        2.0 * math.pi / length
    )
    factor = 1.0 / math.sqrt(length)
    return (jnp.cos(angles) * factor, jnp.sin(angles) * factor)


def apply_table(values, table_in, along_axis):
    rotated = jnp.tensordot(
        values, table_in, axes=((along_axis,), (0,)), precision=lax.Precision.HIGHEST
    )
    return jnp.moveaxis(rotated, -1, along_axis)


def transform(field_in, along_axis, cosine_table, sine_table, phase_sign):
    real_part = field_in[:, :, 0]
    imag_part = field_in[:, :, 1]
    real_cos = apply_table(real_part, cosine_table, along_axis)
    real_sin = apply_table(real_part, sine_table, along_axis)
    imag_cos = apply_table(imag_part, cosine_table, along_axis)
    imag_sin = apply_table(imag_part, sine_table, along_axis)
    return jnp.stack((real_cos - phase_sign * imag_sin, phase_sign * real_sin + imag_cos), axis=2)


def signed_freq(indices, length):
    return jnp.where(indices < length // 2, indices, indices - length).astype(jnp.float32)


def negated(values, along_axis):
    return jnp.roll(jnp.flip(values, along_axis), 1, along_axis)


def products(left_side, right_side):
    band_count = left_side.shape[0]
    highest = lax.Precision.HIGHEST
    left_real = left_side[:, 0].reshape(band_count, -1)
    left_imag = left_side[:, 1].reshape(band_count, -1)
    right_real = right_side[:, 0].reshape(band_count, -1)
    right_imag = right_side[:, 1].reshape(band_count, -1)
    real_sum = jnp.dot(left_real, right_real.T, precision=highest) + jnp.dot(
        left_imag, right_imag.T, precision=highest
    )
    imag_sum = jnp.dot(left_real, right_imag.T, precision=highest) - jnp.dot(
        left_imag, right_real.T, precision=highest
    )
    return (real_sum, imag_sum)


def plain_body(orbitals, responses, energies, weights, potential, perturbation):
    length = orbitals.shape[-1]
    slab_rows = orbitals.shape[3]
    cosine_table, sine_table = tables(length)

    def to_space(field_in):
        return transform(
            transform(field_in, 4, cosine_table, sine_table, 1.0), 3, cosine_table, sine_table, 1.0
        )

    def finish_one(one_piece):
        return transform(one_piece, 2, cosine_table, sine_table, 1.0)

    orbital_space = finish_one(
        lax.all_to_all(to_space(orbitals), "pw", split_axis=4, concat_axis=3, tiled=True)
    )
    response_space = finish_one(
        lax.all_to_all(to_space(responses), "pw", split_axis=4, concat_axis=3, tiled=True)
    )
    partial_value = (
        2.0
        * weights[0]
        * jnp.sum(
            orbital_space[0, :, 0] * response_space[0, :, 0]
            + orbital_space[0, :, 1] * response_space[0, :, 1],
            axis=0,
        )
    )
    applied_space = potential * response_space + perturbation * orbital_space
    first_row = lax.axis_index("pw") * slab_rows
    row_freq = signed_freq(first_row + jnp.arange(slab_rows, dtype=jnp.int32), length)
    full_freq = signed_freq(jnp.arange(length, dtype=jnp.int32), length)
    kinetic = (
        0.5
        * RECIPROCAL_SQUARE
        * (
            row_freq[:, None, None] * row_freq[:, None, None]
            + full_freq[None, :, None] * full_freq[None, :, None]
            + full_freq[None, None, :] * full_freq[None, None, :]
        )
    )
    shifted = kinetic[None] - energies[0][:, None, None, None]
    direct = shifted[None, :, None] * responses
    sectioned = transform(
        transform(applied_space, 4, cosine_table, sine_table, -1.0),
        2,
        cosine_table,
        sine_table,
        -1.0,
    )
    residual = direct + transform(
        lax.all_to_all(sectioned, "pw", split_axis=3, concat_axis=4, tiled=True),
        3,
        cosine_table,
        sine_table,
        -1.0,
    )
    over_real, over_imag = lax.psum(products(orbitals[0], residual[0]), "pw")
    highest = lax.Precision.HIGHEST
    orbital_real = orbitals[0, :, 0]
    orbital_imag = orbitals[0, :, 1]
    combine_real = jnp.einsum(
        "mn,mxyz->nxyz", over_real, orbital_real, precision=highest
    ) - jnp.einsum("mn,mxyz->nxyz", over_imag, orbital_imag, precision=highest)
    combine_imag = jnp.einsum(
        "mn,mxyz->nxyz", over_imag, orbital_real, precision=highest
    ) + jnp.einsum("mn,mxyz->nxyz", over_real, orbital_imag, precision=highest)
    cell_count = float(length**3)
    projected = residual - jnp.stack((combine_real, combine_imag), axis=1)[None] / cell_count
    new_responses = responses - projected / (1.0 + kinetic)[None, None, None]
    summed = lax.psum(partial_value, "pool")
    mirrored = summed + negated(summed, 0)
    row_slab = lax.all_to_all(mirrored, "pw", split_axis=0, concat_axis=1, tiled=True)
    signsum = row_slab + negated(row_slab, 1)
    swapped = lax.all_to_all(signsum, "pw", split_axis=1, concat_axis=0, tiled=True)
    total_sym = signsum + jnp.transpose(swapped, (1, 0, 2))
    return (new_responses, total_sym / 8.0)


def body(orbitals, responses, energies, weights, potential, perturbation):
    slab, length = orbitals.shape[3], orbitals.shape[-1]
    fits = slab == 12 and length == 192 and orbitals.shape[0] == 1 and orbitals.shape[1] == 2
    return (packed_body if fits else plain_body)(
        orbitals, responses, energies, weights, potential, perturbation
    )


def solution(mesh):
    placed = (
        P("pool", None, None, "pw", None, None),
        P("pool", None, None, "pw", None, None),
        P("pool", None),
        P("pool"),
        P(None, "pw", None),
        P(None, "pw", None),
    )
    return jax.shard_map(
        body,
        mesh=mesh,
        in_specs=placed,
        out_specs=(P("pool", None, None, "pw", None, None), P("pw", None, None)),
        check_vma=False,
    )
```

```python
import functools
import math

import jax
import jax.numpy as jnp
import ml_dtypes
import numpy as np
from jax import lax
from jax.experimental import pallas as pl
from jax.experimental.pallas import tpu as pltpu
from jax.sharding import PartitionSpec as P

RECIPROCAL_SQUARE = 0.023428
VMEM_BYTES = 63 * 1024 * 1024


def split_table(table):
    high = table.astype(ml_dtypes.bfloat16)
    low = (table - high.astype(np.float64)).astype(ml_dtypes.bfloat16)
    return np.stack((high, low))


def long_table(table):
    high, low = split_table(table)
    return np.concatenate((high, high, low), axis=1)


def tall_table(table):
    high, low = split_table(table)
    return np.concatenate((high, high, low), axis=0)


@functools.cache
def matrices(length, slab, members):
    index = np.arange(length)
    angles = (index[:, None] * index[None, :] % length) * (2.0 * math.pi / length)
    cosine = np.cos(angles) / math.sqrt(length)
    sine = np.sin(angles) / math.sqrt(length)
    lanes = 128 * -(-length // 128)
    pad = ((0, lanes - length), (0, lanes - length))
    inverse = np.block([[cosine, -sine], [sine, cosine]])
    forward = np.block([[cosine, sine], [-sine, cosine]])
    sent = np.arange(2 * length).reshape(2, members, slab).transpose(1, 0, 2).reshape(-1)
    got = np.arange(2 * length).reshape(2, members, slab // 4, 2, 2).transpose(4, 0, 3, 1, 2)
    got = got.reshape(2, -1)
    first = np.arange(2 * length).reshape(2, 2, length // 2)[:, 0].reshape(-1)
    parity = np.arange(2 * length).reshape(length, 2).T
    mirror = np.eye(length) + np.eye(length)[(-index) % length]
    both = np.zeros((members, 2, slab, 2, length))
    for which in range(2):
        both[:, which, :, which, :] = mirror.reshape(members, slab, length)
    both = both.reshape(2 * length, 2, length)
    alone = np.pad(mirror.reshape(members, slab, length), ((0, 0), (0, 4), (0, 0)))
    alone = alone.reshape(-1, length)
    loose = index.reshape(members, slab).T.reshape(-1)
    fold = np.minimum(index, length - index)
    swapped = np.zeros((2, length, slab + 1, members))
    swapped[0, index, fold % slab, fold // slab] = 1.0
    swapped[0, length // 2] = 0.0
    swapped[0, length // 2, slab, members // 2] = 1.0
    folded = (length - fold) % length
    swapped[1, index, folded % slab, folded // slab] = 1.0
    swapped[1, 0] = 0.0
    swapped[1, 0, slab, 0] = 1.0
    return {
        "cosine": tall_table(np.pad(cosine, pad)),
        "mixed": np.stack(
            [tall_table(np.pad(sine + sign * cosine, pad)) for sign in (-1.0, 1.0)]
        ),
        "inverse_send": np.stack([long_table(inverse[sent[:length]][:, one]) for one in parity]),
        "inverse_receive": np.stack([long_table(inverse[first][:, one]) for one in got]),
        "forward_send": long_table(forward[sent]),
        "forward_receive": np.stack([long_table(forward[first][:, one]) for one in got]),
        "pair": both.reshape(2 * length, -1).astype(ml_dtypes.bfloat16),
        "alone": alone.astype(ml_dtypes.bfloat16),
        "loose_pair": both[:, :, loose].reshape(2 * length, -1).astype(ml_dtypes.bfloat16),
        "loose_alone": alone[:, loose].astype(ml_dtypes.bfloat16),
        "loose_mirror": mirror[:, loose].astype(ml_dtypes.bfloat16),
        "swapped": swapped.reshape(2 * length, -1).astype(ml_dtypes.bfloat16),
    }


def halves(values):
    high = values.astype(jnp.bfloat16)
    return high, (values - high.astype(jnp.float32)).astype(jnp.bfloat16)


def dot(left, right):
    return lax.dot_general(
        left, right, (((1,), (0,)), ((), ())), preferred_element_type=jnp.float32
    )


def dot_right(values, table):
    rows, length = values.shape
    fill = jnp.zeros((rows, table.shape[0] // 3 - length), jnp.float32)
    high, low = halves(jnp.concatenate((values, fill), axis=1))
    return dot(jnp.concatenate((high, low, high), axis=1), table[...])


def dot_left(table, values):
    high, low = halves(values)
    return dot(table, jnp.concatenate((high, low, high), axis=0))


def turn_lanes(real, imag, cosine, mixed, sign):
    common = dot_right(real + imag, cosine)
    if sign > 0:
        return common - dot_right(imag, mixed.at[1]), common + dot_right(real, mixed.at[0])
    return common + dot_right(imag, mixed.at[0]), common - dot_right(real, mixed.at[1])


def half_lengths(even, odd):
    return even + odd, even - odd


def dot_receive(table, found):
    first, second = half_lengths(*(dot_left(table[one], found[one]) for one in range(2)))
    mid = first.shape[0] // 2
    return (
        jnp.concatenate((first[:mid], second[:mid]), axis=0),
        jnp.concatenate((first[mid:], second[mid:]), axis=0),
    )


def dot_mirror(table, values):
    high, low = halves(values)
    return dot(table, high) + dot(table, low)


def merge_tails(first, second):
    return first + pltpu.roll(second, 64, 1)


def to_half_kernel(field, cosine, mixed, send, out, turned):
    pair, length = field.shape[3], field.shape[4]
    members, rows = out.shape[0], out.shape[-2]
    mid = members // 2
    out = out.at[:, 0, 0]
    parts = [field[0, 0, part].reshape(pair * length, length) for part in range(2)]
    parts = turn_lanes(*parts, cosine, mixed, 1)
    for part in range(2):
        turned[part, 0] = parts[part][:, :128]
        turned[part, 1] = parts[part][:, 128:]
    tails = []
    for one in range(pair):
        found = []
        for parity in range(2):
            rows_of = pl.ds(one * length + parity, length // 2, stride=2)
            found.append(
                jnp.concatenate(
                    [
                        jnp.concatenate((turned[part, 0, rows_of], turned[part, 1, rows_of]), axis=1)
                        for part in range(2)
                    ],
                    axis=0,
                )
            )
        done = half_lengths(*(dot_left(send[parity], found[parity]) for parity in range(2)))
        for half in range(2):
            to = slice(half * mid, (half + 1) * mid)
            out[to, one] = done[half][:, :128].reshape(mid, rows, 128)
        tails.append([piece[:, 128:] for piece in done])
    for half in range(2):
        to = slice(half * mid, (half + 1) * mid)
        out[to, 2] = merge_tails(tails[0][half], tails[1][half]).reshape(mid, rows, 128)


def received(ref, start, stride, count):
    return ref[pl.ds(start, count, stride=stride), :]


def plane(parts_of, place, slab, with_main, with_tail):
    def rows_at(row):
        pieces = [
            received(ref, start + row, stride, ref.shape[0] // stride)
            for ref, start, stride in parts_of
        ]
        return jnp.concatenate(pieces, axis=0)

    found = [[], []]
    for part in range(2):
        row = part * slab + place
        mains, tails = [None, None], [None, None]
        if with_main:
            mains = [rows_at(one * 2 * slab + row) for one in range(2)]
            row = row + 4 * slab
        if with_tail:
            tail = rows_at(row)
            tails = [tail, pltpu.roll(tail, 64, 1)]
        for one in range(2):
            pieces = [piece for piece in (mains[one], tails[one]) if piece is not None]
            found[one].append(jnp.concatenate(pieces, axis=1) if len(pieces) > 1 else pieces[0])
    return [jnp.concatenate(one, axis=0) for one in found]


def to_space_kernel(slab, starts, strides, *refs):
    *gots, receive, space = refs
    length = space.shape[2]
    parts_of = list(zip(gots if len(gots) > 1 else gots * 2, starts, strides))
    for one in range(2):
        place = 2 * pl.program_id(0) + one
        values = plane(parts_of, place, slab, True, True)
        real, imag = dot_receive(receive, values)
        space[one, :length] = real[:, :length]
        space[one, length:] = imag[:, :length]


def folded(values):
    return values.reshape(-1, 8, values.shape[-1]).sum(axis=0)


def apply_kernel(
    slab, starts, stride, band, weights, got, spaces, potential, perturbation, before,
    receive, cosine, mixed, send, out_main, out_tail, inner, density
):
    length = potential.shape[1]
    members, rows = out_main.shape[0], out_main.shape[3]
    step = pl.program_id(0)
    twice_weight = 2.0 * weights[0]

    @pl.when(step == 0)
    def _():
        inner[...] = jnp.zeros_like(inner)

    tails = []
    sums = []
    for one in range(2):
        parts_of = [(got, start, stride) for start in starts]
        values = plane(parts_of, 2 * step + one, slab, True, True)
        real, imag = (piece[:, :length] for piece in dot_receive(receive, values))
        own_real, own_imag = spaces[band, one, :length], spaces[band, one, length:]
        local = twice_weight * (own_real * real + own_imag * imag)
        if before is not None:
            local = local + before[one]
        sums.append(local)
        field, change = potential[one], perturbation[one]
        real = field * real + change * own_real
        imag = field * imag + change * own_imag
        for other in range(2):
            left_real, left_imag = spaces[other, one, :length], spaces[other, one, length:]
            inner[0, other] += folded(left_real * real + left_imag * imag)
            inner[1, other] += folded(left_real * imag - left_imag * real)
        turned = jnp.concatenate(turn_lanes(real, imag, cosine, mixed, -1), axis=0)
        done = dot_left(send[...], turned)
        out_main[:, 0, one] = done[:, :128].reshape(members, rows, 128)
        tails.append(done[:, 128:])
    tail = merge_tails(*tails).reshape(members, rows, 128)
    if out_tail is None:
        out_main[:, 0, 2] = tail
    else:
        out_tail[:, 0] = tail
    for one in range(2):
        density[one] = sums[one]


def lanes_of(values):
    return lax.broadcasted_iota(jnp.int32, values.shape, 1)


def moved(values, by):
    return pltpu.roll(values, by % 128, 1) if by % 128 else values


def pack(planes, count, width, pair, alone, out):
    members = out.shape[0]
    blocks = []
    for block in range(-(-count * width // 128)):
        made = None
        for place in range(count):
            start = place * width - 128 * block
            if start >= 128 or start + width <= 0:
                continue
            values = moved(planes(place), start)
            made = values if made is None else jnp.where(lanes_of(values) < start, made, values)
        blocks.append(made)
    for first in range(0, len(blocks) - 1, 2):
        out[:, 12 * first : 12 * first + 24] = dot_mirror(
            pair[...], jnp.concatenate(blocks[first : first + 2], axis=0)
        ).reshape(members, 24, 128)
    out[:, 12 * len(blocks) - 12 :] = dot_mirror(alone[...], blocks[-1]).reshape(members, 16, 128)


def unpack(got, place, count, width, rows, row_at=lambda row: row):
    members = got.shape[0] // rows
    blocks = [
        received(got, row_at(12 * block + place), rows, members)
        for block in range(-(-count * width // 128))
    ]
    found = []
    for one in range(count):
        block, start = divmod(one * width, 128)
        values = moved(blocks[block], -start)
        if start + width > 128:
            rest = moved(blocks[block + 1], -start)
            values = jnp.where(lanes_of(values) < 128 - start, values, rest)
        found.append(values)
    return jnp.concatenate(found, axis=0)


def pack_kernel(pool, density, pair, alone, kept, given):
    length = density.shape[1]
    own = pool[0] == 0

    def one_half(which):
        def planes(place):
            low = density[place, :, :128]
            rest = jnp.concatenate(
                (density[place, :, 128:], jnp.zeros((length, 64), jnp.float32)), axis=1
            )
            high = jnp.where(lanes_of(low) < 32, moved(low, 32), moved(rest, 32))
            return jnp.where(own, low, high) if which else jnp.where(own, high, low)

        return planes

    pack(one_half(True), 12, 96, pair, alone, kept)
    pack(one_half(False), 12, 96, pair, alone, given)


def frequencies(length, first, lanes, first_lane):
    rows = lax.broadcasted_iota(jnp.int32, (length, lanes), 0)
    columns = lax.broadcasted_iota(jnp.int32, (length, lanes), 1) + first_lane
    row = jnp.where(rows < length // 2, rows, rows - length).astype(jnp.float32)
    column = jnp.where(columns < length // 2, columns, columns - length).astype(jnp.float32)
    outer = jnp.where(first < length // 2, first, first - length).astype(jnp.float32)
    return 0.5 * RECIPROCAL_SQUARE * (outer * outer + row * row + column * column)


def inner_kernel(slab, me, energies, orbitals, responses, inner):
    length = orbitals.shape[4]
    step = pl.program_id(0)

    @pl.when(step == 0)
    def _():
        inner[...] = jnp.zeros_like(inner)

    for one in range(2):
        kinetic = frequencies(length, me[0] * slab + 2 * step + one, length, 0)
        for band in range(2):
            shifted = kinetic - energies[0, band]
            real = shifted * responses[0, band, 0, one]
            imag = shifted * responses[0, band, 1, one]
            for other in range(2):
                left_real, left_imag = orbitals[0, other, 0, one], orbitals[0, other, 1, one]
                inner[0, other, band] += folded(left_real * real + left_imag * imag)
                inner[1, other, band] += folded(left_real * imag - left_imag * real)


def direct_kernel(slab, me, energies, inner, orbitals, responses, out):
    length = orbitals.shape[4]
    cells = float(length**3)
    for one in range(2):
        kinetic = frequencies(length, me[0] * slab + 2 * pl.program_id(0) + one, length, 0)
        inverse = 1.0 / (1.0 + kinetic)
        for band in range(2):
            shifted = kinetic - energies[0, band]
            real = shifted * responses[0, band, 0, one]
            imag = shifted * responses[0, band, 1, one]
            for other in range(2):
                left_real, left_imag = orbitals[0, other, 0, one], orbitals[0, other, 1, one]
                by_real = inner[0, other, band] / cells
                by_imag = inner[1, other, band] / cells
                real = real - (left_real * by_real - left_imag * by_imag)
                imag = imag - (left_real * by_imag + left_imag * by_real)
            out[0, band, 0, one] = responses[0, band, 0, one] - real * inverse
            out[0, band, 1, one] = responses[0, band, 1, one] - imag * inverse


def finish_kernel(slab, starts, stride, tail, me, got, receive, base, out):
    length, count = base.shape[4], base.shape[3]
    parts_of = [(got, start, stride) for start in starts]
    for pair in range(0, count, 2):
        first = count * pl.program_id(0) + pair
        planes = [plane(parts_of, first + one, slab, not tail, tail) for one in range(2)]
        values = [jnp.concatenate(both, axis=1) for both in zip(*planes)]
        applied = dot_receive(receive, values)
        for one in range(2):
            kinetic = frequencies(length, me[0] * slab + first + one, 128, 128 if tail else 0)
            inverse = 1.0 / (1.0 + kinetic)
            for part in range(2):
                piece = applied[part][:, 128 * one : 128 * (one + 1)]
                out[0, 0, part, pair + one] = base[0, 0, part, pair + one] - piece * inverse


def mixed_row(row):
    return row // 40 * 88 + 48 + row % 40


def mirror_kernel(me, got, pair, alone, out, loose):
    below = me[0] < out.shape[0] // 2
    for place in range(12):
        loose[place] = unpack(got, place, 12, 96, 264, mixed_row)

    def planes(place):
        values = loose[place % 12]
        other = moved(values, -48)
        return jnp.where(below, values, other) if place < 12 else jnp.where(below, other, values)

    pack(planes, 13, 48, pair, alone, out)


def swap_kernel(got, got_swapped, single, order, out):
    length = out.shape[1]
    for place in range(12):
        own = dot_mirror(single[...], unpack(got, place, 12, 96, 264, mixed_row))
        halves_of = dot_mirror(order[...], unpack(got_swapped, place, 13, 48, 64))
        low, high = halves_of[:length], moved(halves_of[length:], 48)
        swapped = jnp.where(lanes_of(low) < 48, low, high)
        out[place] = (own + swapped) * 0.125


def cost(flops, moved):
    return pl.CostEstimate(flops=int(flops), bytes_accessed=int(moved), transcendentals=0)


def whole():
    return pl.BlockSpec(memory_space=pltpu.VMEM)


def scalars():
    return pl.BlockSpec(memory_space=pltpu.SMEM)


def call(kernel, name, grid, ins, outs, shapes, estimate, aliases=None, scratch=()):
    return pl.pallas_call(
        kernel,
        grid=(grid,),
        in_specs=ins,
        out_specs=outs,
        out_shape=shapes,
        compiler_params=pltpu.CompilerParams(
            dimension_semantics=("arbitrary",), vmem_limit_bytes=VMEM_BYTES
        ),
        cost_estimate=estimate,
        input_output_aliases=aliases or {},
        scratch_shapes=scratch,
        name=name,
    )


def f32(*shape):
    return jax.ShapeDtypeStruct(shape, jnp.float32)


def packed_body(orbitals, responses, energies, weights, potential, perturbation):
    length = orbitals.shape[-1]
    slab = orbitals.shape[3]
    members = length // slab
    pairs = slab // 2
    rows = 2 * slab
    table = {key: jnp.asarray(value) for key, value in matrices(length, slab, members).items()}
    me = lax.axis_index("pw").astype(jnp.int32).reshape(1)
    pool = lax.axis_index("pool").astype(jnp.int32).reshape(1)
    field_bytes = 4 * members * pairs * 3 * rows * 128
    stage_flops = 6 * 2 * 2 * length * length * length * slab * 2

    half_spec = pl.BlockSpec((members, 1, 3, rows, 128), lambda p: (0, p, 0, 0, 0))
    half_shape = f32(members, pairs, 3, rows, 128)

    def exchange(values, after=None):
        values = values.reshape(members, -1, 128)
        if after is not None:
            values, _ = lax.optimization_barrier((values, after))
        return lax.all_to_all(values, "pw", split_axis=0, concat_axis=0, tiled=True)

    def to_half(field, band, slots, group=None, into=None, slot=0):
        def kernel(field, cosine, mixed, send, *rest):
            to_half_kernel(field, cosine, mixed, send, *rest[-2:])

        if group is None:
            grid = pairs
            pair_at = lambda p: p
            block_at = lambda p: (0, p // 2, slot + p % 2, 0, 0, 0)
        else:
            grid = pairs // 2
            pair_at = lambda p: 2 * p + group
            block_at = lambda p: (0, p, slot, 0, 0, 0)
        return call(
            kernel,
            "to_half",
            grid,
            [
                pl.BlockSpec(
                    (1, 1, 2, 2, length, length), lambda p: (0, band, 0, pair_at(p), 0, 0)
                ),
                whole(),
                whole(),
                whole(),
            ]
            + ([] if into is None else [pl.BlockSpec(memory_space=pl.ANY)]),
            pl.BlockSpec((members, 1, 1, 3, rows, 128), block_at),
            f32(members, pairs // 2, slots, 3, rows, 128),
            cost(2 * stage_flops * grid / pairs, 2 * field_bytes * grid / pairs),
            {} if into is None else {4: 0},
            [pltpu.VMEM((2, 2, 2 * length, 128), jnp.float32)],
        )(
            field, table["cosine"], table["mixed"], table["inverse_send"],
            *(() if into is None else (into,)),
        )

    def to_space(gots, starts, strides):
        return call(
            functools.partial(to_space_kernel, slab, starts, strides),
            "to_space",
            pairs,
            [whole()] * (len(gots) + 1),
            pl.BlockSpec((2, 2 * length, length), lambda p: (p, 0, 0)),
            f32(slab, 2 * length, length),
            cost(stage_flops, 2 * field_bytes),
        )(*(got.reshape(-1, 128) for got in gots), table["inverse_receive"])

    plane_spec = pl.BlockSpec((2, length, length), lambda p: (p, 0, 0))
    send_specs = [
        pl.BlockSpec((members, 1, 2, rows, 128), lambda p: (0, p, 0, 0, 0)),
        pl.BlockSpec((members, 1, rows, 128), lambda p: (0, p, 0, 0)),
    ]
    send_shapes = [
        f32(members, pairs, 2, rows, 128),
        f32(members, pairs, rows, 128),
    ]
    block_shape = f32(members, 112, 128)
    inner_spec = pl.BlockSpec((2, 2, 8, length), lambda p: (0, 0, 0, 0))

    def apply_first(got, spaces, field, change):
        def kernel(weights, got, first, second, field, change, *tables_and_outs):
            receive, cosine, mixed, send, main, inner, density = tables_and_outs
            apply_kernel(
                slab, (9 * rows, 12 * rows), 15 * rows, 0, weights, got, Both(first, second), field, change, None,
                receive, cosine, mixed, send, main, None, inner, density,
            )

        return call(
            kernel,
            "apply_first",
            pairs,
            [scalars(), whole(), space_spec, space_spec, plane_spec, plane_spec] + [whole()] * 4,
            [half_spec, inner_spec, plane_spec],
            [half_shape, f32(2, 2, 8, length), f32(slab, length, length)],
            cost(3 * stage_flops, 5 * field_bytes),
        )(
            weights, got.reshape(-1, 128), *spaces, field, change,
            table["inverse_receive"], table["cosine"], table["mixed"], table["forward_send"],
        )

    def apply_last(got, spaces, field, change, before):
        def kernel(weights, got, first, second, field, change, before, *tables_and_outs):
            receive, cosine, mixed, send, main, tail, inner, density = tables_and_outs
            apply_kernel(
                slab, (0, 3 * rows), 6 * rows, 1, weights, got, Both(first, second), field, change, before,
                receive, cosine, mixed, send, main, tail, inner, density,
            )

        return call(
            kernel,
            "apply_last",
            pairs,
            [scalars(), whole(), space_spec, space_spec] + [plane_spec] * 3 + [whole()] * 4,
            send_specs + [inner_spec, plane_spec],
            send_shapes + [f32(2, 2, 8, length), f32(slab, length, length)],
            cost(3 * stage_flops, 5 * field_bytes),
        )(
            weights, got.reshape(-1, 128), *spaces, field, change, before,
            table["inverse_receive"], table["cosine"], table["mixed"], table["forward_send"],
        )

    space_spec = pl.BlockSpec((2, 2 * length, length), lambda p: (p, 0, 0))
    bands_spec = pl.BlockSpec((1, 2, 2, 2, length, length), lambda p: (0, 0, 0, p, 0, 0))

    def finish(base, got, band, starts, stride, tail):
        lane_block = 1 if tail else 0
        one_spec = pl.BlockSpec(
            (1, 1, 2, slab // 2, length, 128), lambda p: (0, band, 0, p, 0, lane_block)
        )
        return call(
            functools.partial(finish_kernel, slab, starts, stride, tail),
            "finish",
            2,
            [scalars(), whole(), whole(), one_spec],
            one_spec,
            f32(*base.shape),
            cost(stage_flops, 2 * field_bytes),
            {3: 0},
        )(me, got.reshape(-1, 128), table["forward_receive"], base)

    field = jnp.transpose(potential, (1, 0, 2))
    change = jnp.transpose(perturbation, (1, 0, 2))
    got_one = exchange(to_half(orbitals, 0, 1, 0))
    half_two = to_half(orbitals, 0, 5, 1)
    half_two = to_half(orbitals, 1, 5, None, half_two, 1)
    got_two = exchange(to_half(responses, 0, 5, None, half_two, 3), got_one)
    direct_inner = call(
        functools.partial(inner_kernel, slab),
        "inner",
        pairs,
        [scalars(), scalars(), bands_spec, bands_spec],
        pl.BlockSpec((2, 2, 2, 8, length), lambda p: (0, 0, 0, 0, 0)),
        f32(2, 2, 2, 8, length),
        cost(32 * field_bytes, 4 * field_bytes),
    )(me, energies, orbitals, responses)
    got_last = exchange(to_half(responses, 1, 2), (got_two, direct_inner))
    spaces = [
        to_space([got_one, got_two], (0, 0), (3 * rows, 15 * rows)),
        to_space([got_two], (3 * rows, 6 * rows), (15 * rows, 15 * rows)),
    ]
    send_first, inner_first, before = apply_first(got_two, spaces, field, change)
    back_first = exchange(send_first, got_last)
    last_main, last_tail, inner_last, density = apply_last(
        got_last, spaces, field, change, before
    )
    kept, given = call(
        pack_kernel,
        "pack",
        1,
        [scalars(), whole(), whole(), whole()],
        [whole(), whole()],
        [block_shape, block_shape],
        cost(4e9, 5e6),
    )(pool, density, table["pair"], table["alone"])
    swap = [(0, 1), (1, 0)]
    local_inner = direct_inner + jnp.stack((inner_first, inner_last), axis=2)
    riding = jnp.sum(local_inner, axis=(3, 4)).reshape(1, 1, 8)
    riding = jnp.pad(riding, ((0, 0), (0, 0), (0, 120)))
    row = lax.broadcasted_iota(jnp.int32, block_shape.shape, 1)
    summed = jnp.where(row < 108, kept + lax.ppermute(given, "pool", swap), riding)
    summed = jnp.pad(summed, ((0, 0), (0, 8), (0, 0))).reshape(members, 3, 40, 128)
    mixed = jnp.concatenate((last_tail.reshape(members, 3, 48, 128), summed), axis=2)
    got_mixed = exchange(mixed, back_first)
    inner = jnp.sum(got_mixed[:, mixed_row(108), :8], axis=0).reshape(2, 2, 2)
    base = call(
        functools.partial(direct_kernel, slab),
        "direct",
        pairs,
        [scalars(), scalars(), scalars(), bands_spec, bands_spec],
        bands_spec,
        f32(*responses.shape),
        cost(32 * field_bytes, 6 * field_bytes),
    )(me, energies, inner, orbitals, responses)
    mirrored = call(
        mirror_kernel,
        "mirror",
        1,
        [scalars()] + [whole()] * 3,
        whole(),
        f32(members, 64, 128),
        cost(2e9, 3e6),
        scratch=[pltpu.VMEM((slab, length, 128), jnp.float32)],
    )(me, got_mixed.reshape(-1, 128), table["loose_pair"], table["loose_alone"])
    got_mirrored = exchange(mirrored)
    base = finish(base, back_first, 0, (0, 3 * rows), 6 * rows, False)
    back_main = exchange(last_main, got_mirrored)
    symmetric = call(
        swap_kernel,
        "swap",
        1,
        [whole()] * 4,
        whole(),
        f32(slab, length, 128),
        cost(2e9, 5e6),
    )(
        got_mixed.reshape(-1, 128), got_mirrored.reshape(-1, 128),
        table["loose_mirror"], table["swapped"],
    )
    other = lax.ppermute(symmetric, "pool", swap)
    low = jnp.where(pool == 0, symmetric, other)
    high = jnp.where(pool == 0, other, symmetric)
    response_density = jnp.concatenate((low[..., :96], high[..., :96]), axis=2)
    base = finish(base, back_first, 0, (2 * rows, 5 * rows), 6 * rows, True)
    base = finish(base, got_mixed, 1, (0, rows), 88, True)
    base, response_density, back_main = lax.optimization_barrier(
        (base, response_density, back_main)
    )
    base = finish(base, back_main, 1, (0, 2 * rows), 4 * rows, False)
    return base, response_density


class Both:
    def __init__(self, *refs):
        self.refs = refs

    def __getitem__(self, index):
        return self.refs[index[0]][index[1:]]


def tables(length):
    indices = jnp.arange(length, dtype=jnp.int32)
    angles = (indices[:, None] * indices[None, :] % length).astype(jnp.float32) * (
        2.0 * math.pi / length
    )
    factor = 1.0 / math.sqrt(length)
    return (jnp.cos(angles) * factor, jnp.sin(angles) * factor)


def apply_table(values, table_in, along_axis):
    rotated = jnp.tensordot(
        values, table_in, axes=((along_axis,), (0,)), precision=lax.Precision.HIGHEST
    )
    return jnp.moveaxis(rotated, -1, along_axis)


def transform(field_in, along_axis, cosine_table, sine_table, phase_sign):
    real_part = field_in[:, :, 0]
    imag_part = field_in[:, :, 1]
    real_cos = apply_table(real_part, cosine_table, along_axis)
    real_sin = apply_table(real_part, sine_table, along_axis)
    imag_cos = apply_table(imag_part, cosine_table, along_axis)
    imag_sin = apply_table(imag_part, sine_table, along_axis)
    return jnp.stack((real_cos - phase_sign * imag_sin, phase_sign * real_sin + imag_cos), axis=2)


def signed_freq(indices, length):
    return jnp.where(indices < length // 2, indices, indices - length).astype(jnp.float32)


def negated(values, along_axis):
    return jnp.roll(jnp.flip(values, along_axis), 1, along_axis)


def products(left_side, right_side):
    band_count = left_side.shape[0]
    highest = lax.Precision.HIGHEST
    left_real = left_side[:, 0].reshape(band_count, -1)
    left_imag = left_side[:, 1].reshape(band_count, -1)
    right_real = right_side[:, 0].reshape(band_count, -1)
    right_imag = right_side[:, 1].reshape(band_count, -1)
    real_sum = jnp.dot(left_real, right_real.T, precision=highest) + jnp.dot(
        left_imag, right_imag.T, precision=highest
    )
    imag_sum = jnp.dot(left_real, right_imag.T, precision=highest) - jnp.dot(
        left_imag, right_real.T, precision=highest
    )
    return (real_sum, imag_sum)


def plain_body(orbitals, responses, energies, weights, potential, perturbation):
    length = orbitals.shape[-1]
    slab_rows = orbitals.shape[3]
    cosine_table, sine_table = tables(length)

    def to_space(field_in):
        return transform(
            transform(field_in, 4, cosine_table, sine_table, 1.0), 3, cosine_table, sine_table, 1.0
        )

    def finish_one(one_piece):
        return transform(one_piece, 2, cosine_table, sine_table, 1.0)

    orbital_space = finish_one(
        lax.all_to_all(to_space(orbitals), "pw", split_axis=4, concat_axis=3, tiled=True)
    )
    response_space = finish_one(
        lax.all_to_all(to_space(responses), "pw", split_axis=4, concat_axis=3, tiled=True)
    )
    partial_value = (
        2.0
        * weights[0]
        * jnp.sum(
            orbital_space[0, :, 0] * response_space[0, :, 0]
            + orbital_space[0, :, 1] * response_space[0, :, 1],
            axis=0,
        )
    )
    applied_space = potential * response_space + perturbation * orbital_space
    first_row = lax.axis_index("pw") * slab_rows
    row_freq = signed_freq(first_row + jnp.arange(slab_rows, dtype=jnp.int32), length)
    full_freq = signed_freq(jnp.arange(length, dtype=jnp.int32), length)
    kinetic = (
        0.5
        * RECIPROCAL_SQUARE
        * (
            row_freq[:, None, None] * row_freq[:, None, None]
            + full_freq[None, :, None] * full_freq[None, :, None]
            + full_freq[None, None, :] * full_freq[None, None, :]
        )
    )
    shifted = kinetic[None] - energies[0][:, None, None, None]
    direct = shifted[None, :, None] * responses
    sectioned = transform(
        transform(applied_space, 4, cosine_table, sine_table, -1.0),
        2,
        cosine_table,
        sine_table,
        -1.0,
    )
    residual = direct + transform(
        lax.all_to_all(sectioned, "pw", split_axis=3, concat_axis=4, tiled=True),
        3,
        cosine_table,
        sine_table,
        -1.0,
    )
    over_real, over_imag = lax.psum(products(orbitals[0], residual[0]), "pw")
    highest = lax.Precision.HIGHEST
    orbital_real = orbitals[0, :, 0]
    orbital_imag = orbitals[0, :, 1]
    combine_real = jnp.einsum(
        "mn,mxyz->nxyz", over_real, orbital_real, precision=highest
    ) - jnp.einsum("mn,mxyz->nxyz", over_imag, orbital_imag, precision=highest)
    combine_imag = jnp.einsum(
        "mn,mxyz->nxyz", over_imag, orbital_real, precision=highest
    ) + jnp.einsum("mn,mxyz->nxyz", over_real, orbital_imag, precision=highest)
    cell_count = float(length**3)
    projected = residual - jnp.stack((combine_real, combine_imag), axis=1)[None] / cell_count
    new_responses = responses - projected / (1.0 + kinetic)[None, None, None]
    summed = lax.psum(partial_value, "pool")
    mirrored = summed + negated(summed, 0)
    row_slab = lax.all_to_all(mirrored, "pw", split_axis=0, concat_axis=1, tiled=True)
    signsum = row_slab + negated(row_slab, 1)
    swapped = lax.all_to_all(signsum, "pw", split_axis=1, concat_axis=0, tiled=True)
    total_sym = signsum + jnp.transpose(swapped, (1, 0, 2))
    return (new_responses, total_sym / 8.0)


def body(orbitals, responses, energies, weights, potential, perturbation):
    slab, length = orbitals.shape[3], orbitals.shape[-1]
    fits = slab == 12 and length == 192 and orbitals.shape[0] == 1 and orbitals.shape[1] == 2
    return (packed_body if fits else plain_body)(
        orbitals, responses, energies, weights, potential, perturbation
    )


def solution(mesh):
    placed = (
        P("pool", None, None, "pw", None, None),
        P("pool", None, None, "pw", None, None),
        P("pool", None),
        P("pool"),
        P(None, "pw", None),
        P(None, "pw", None),
    )
    return jax.shard_map(
        body,
        mesh=mesh,
        in_specs=placed,
        out_specs=(P("pool", None, None, "pw", None, None), P("pw", None, None)),
        check_vma=False,
    )
```
